256 devices in a mesh: section: 2 (over core), dp: 32 (over z, x), head: 4 (over y).
Axes of the slice: x: 4, y: 4, z: 8, core: 2. Of those that a mesh axis runs over, the one named last changes fastest.
Arguments:
- stream: bfloat16 [2, 32, 128, 4096], P(None, 'dp', None, 'head'), may hold values from -6 to 6
- norm_gain: float32 [2, 4096], P('section'), may hold values from 0.1 to 1.9
- w_x: bfloat16 [2, 4096, 4096], P('section', 'dp', 'head'), may hold values from -0.09375 to 0.09375
- w_bc: bfloat16 [2, 4096, 1024], P('section', 'dp', 'head'), may hold values from -0.09375 to 0.09375
- w_dt: bfloat16 [2, 4096, 64], P('section', 'dp', 'head'), may hold values from -0.09375 to 0.09375
- conv_x: float32 [2, 4, 4096], P('section', None, 'head'), may hold values from -3 to 3
- conv_bc: float32 [2, 4, 1024], P('section', None, 'head'), may hold values from -3 to 3
- dt_bias: float32 [2, 64], P('section', 'head'), may hold values from -3 to -1
- decay_rate: float32 [2, 64], P('section', 'head'), may hold values from 0.25 to 16
- skip_d: float32 [2, 64], P('section', 'head'), may hold values from 0.5 to 2
- y_gain: float32 [2, 4096], P('section', 'head'), may hold values from 0.1 to 1.9
- w_out: bfloat16 [2, 4096, 4096], P('section', 'head', 'dp'), may hold values from -0.09375 to 0.09375
Outputs:
- states: bfloat16 [2, 2, 32, 128, 4096], P('section', None, 'dp', None, 'head')
The draws below stay inside these ranges and needn't reach their ends.
All inputs are finite; a program needn't handle non-finite values.
Results may differ from the reference program's by a relative error of at most 0.018.
Values may be sent and summed in bfloat16 or wider, within the bound.
A program may use at most 64 MiB of HBM per device.

```python
import math
import jax
import jax.numpy as jnp
from jax import lax

D = 4096
HEADS = 64
HEAD_DIM = 64
STATE = 128
GROUPS = 4
KW = 4
LEN = 128
MICRO = 2
INNER = 4096
BCW = 1024
LAYERS = 2
SEQS = 32
SHARDS = 4


def block_scale(key, extent, shards, smallest, largest):
    loudness = 1.0
    for position, shards_of in shards:
        steps = jax.random.uniform(jax.random.fold_in(jax.random.fold_in(key, 6), position), (shards_of,), jnp.float32, smallest / len(shards), largest / len(shards))
        loudness = loudness * jnp.repeat(jnp.exp(steps), extent[position] // shards_of).reshape((-1,) + (1,) * (len(extent) - 1 - position))
    return loudness


def centred(own_key, extent, deviation, reach, split=(), dtype=jnp.bfloat16):
    loudness = block_scale(own_key, extent, split, -0.22, 0.18) if split else 1.0
    result = jax.random.normal(own_key, extent, jnp.float32) * deviation * loudness
    return jnp.minimum(jnp.maximum(result, -reach), reach).astype(dtype)


def setup_inputs(seed: int = 0) -> dict:
    streams_of = jax.random.split(jax.random.key(seed), 13)
    return {
        "stream": centred(streams_of[0], (MICRO, SEQS, LEN, D), 1.0, 6.0, ((1, 32), (3, 4))),
        "norm_gain": jnp.clip(1.0 + 0.18 * jax.random.normal(streams_of[1], (LAYERS, D), jnp.float32), 0.1, 1.9),
        "w_x": centred(streams_of[2], (LAYERS, D, INNER), D ** -0.5, 0.09375, ((0, 2), (1, 32), (2, 4))),
        "w_bc": centred(streams_of[3], (LAYERS, D, BCW), D ** -0.5, 0.09375, ((0, 2), (1, 32), (2, 4))),
        "w_dt": centred(streams_of[4], (LAYERS, D, HEADS), D ** -0.5, 0.09375, ((0, 2), (1, 32), (2, 4))),
        "conv_x": centred(streams_of[5], (LAYERS, KW, INNER), 0.5, 3.0, ((0, 2), (2, 4)), jnp.float32),
        "conv_bc": centred(streams_of[6], (LAYERS, KW, BCW), 0.5, 3.0, ((0, 2), (2, 4)), jnp.float32),
        "dt_bias": jnp.clip(-3.0 + 2.0 * jax.random.uniform(streams_of[7], (LAYERS, HEADS), jnp.float32) ** block_scale(streams_of[7], (LAYERS, HEADS), ((0, 2), (1, 4)), -0.2, 0.2), -3.0, -1.0),
        "decay_rate": jnp.clip(jnp.exp(math.log(16.0) - 4.158883 * jax.random.uniform(streams_of[8], (LAYERS, HEADS), jnp.float32) ** block_scale(streams_of[8], (LAYERS, HEADS), ((0, 2), (1, 4)), -0.2, 0.2)), 0.25, 16.0),
        "skip_d": jnp.clip(0.5 + 1.5 * jax.random.uniform(streams_of[9], (LAYERS, HEADS), jnp.float32) ** block_scale(streams_of[9], (LAYERS, HEADS), ((0, 2), (1, 4)), -0.2, 0.2), 0.5, 2.0),
        "y_gain": jnp.clip(1.0 + 0.18 * jax.random.normal(streams_of[10], (LAYERS, INNER), jnp.float32), 0.1, 1.9),
        "w_out": centred(streams_of[11], (LAYERS, INNER, D), INNER ** -0.5, 0.09375, ((0, 2), (1, 4), (2, 32))),
    }


def causal_conv(values, kernel):
    kernel_width = kernel.shape[0]
    length = values.shape[-2]
    widths = [(0, 0)] * (values.ndim - 2) + [(kernel_width - 1, 0), (0, 0)]
    padded = jnp.pad(values, widths)
    summed = jnp.zeros_like(values)
    for tap in range(kernel_width):
        summed = summed + kernel[tap] * padded[..., tap:tap + length, :]
    return jax.nn.silu(summed)

def apply_layer(h_in, layer_index, norm_gain, w_x, w_bc, w_dt, conv_x, conv_bc, dt_bias, decay_rate, skip_d, y_gain, w_out):
    row_count = h_in.shape[0]
    per_group = HEADS // GROUPS
    h_float = h_in.astype(jnp.float32)
    normed = h_float * lax.rsqrt(lax.optimization_barrier(jnp.mean(h_float * h_float, axis=-1, keepdims=True)) + 1e-05) * norm_gain[layer_index]
    flat = normed.astype(jnp.bfloat16).reshape(row_count * LEN, D)
    x_proj = jnp.dot(flat, w_x[layer_index], preferred_element_type=jnp.float32).reshape(row_count, LEN, INNER)
    bc_proj = jnp.dot(flat, w_bc[layer_index], preferred_element_type=jnp.float32).reshape(row_count, LEN, BCW)
    dt_raw = jnp.dot(flat, w_dt[layer_index], preferred_element_type=jnp.float32).reshape(row_count, LEN, HEADS)
    x_conv = causal_conv(x_proj, conv_x[layer_index])
    bc_conv = causal_conv(bc_proj, conv_bc[layer_index])
    step_size = jax.nn.softplus(dt_raw + dt_bias[layer_index])
    bc_split = bc_conv.reshape(row_count, LEN, GROUPS, 2, STATE)
    b_state = bc_split[:, :, :, 0, :]
    c_state = bc_split[:, :, :, 1, :]
    cb_scores = jnp.einsum('rtgn,rsgn->rtsg', c_state, b_state, precision=lax.Precision.HIGHEST)
    decay_sum = jnp.cumsum(step_size * decay_rate[layer_index], axis=1)
    decay_gap = decay_sum[:, :, None, :] - decay_sum[:, None, :, :]
    causal_mask = (jnp.arange(LEN)[:, None] >= jnp.arange(LEN)[None, :])[None, :, :, None]
    kernel_mix = jnp.where(causal_mask, jnp.exp(-jnp.where(causal_mask, decay_gap, 0.0)), 0.0)
    kernel_mix = kernel_mix.reshape(row_count, LEN, LEN, GROUPS, per_group)
    mixing = cb_scores[:, :, :, :, None] * kernel_mix * step_size.reshape(row_count, 1, LEN, GROUPS, per_group)
    x_heads = x_conv.reshape(row_count, LEN, GROUPS, per_group, HEAD_DIM)
    y_heads = jnp.einsum('rtsgj,rsgjp->rtgjp', mixing, x_heads, precision=lax.Precision.HIGHEST)
    y_heads = y_heads + skip_d[layer_index].reshape(GROUPS, per_group)[None, None, :, :, None] * x_heads
    y_group = y_heads.reshape(row_count, LEN, GROUPS, per_group * HEAD_DIM)
    y_group = y_group * lax.rsqrt(lax.optimization_barrier(jnp.mean(y_group * y_group, axis=-1, keepdims=True)) + 1e-05)
    y_normed = (y_group.reshape(row_count, LEN, INNER) * y_gain[layer_index]).astype(jnp.bfloat16)
    y_flat = y_normed.reshape(row_count * LEN, INNER)
    block = INNER // SHARDS
    summed = jnp.zeros((row_count * LEN, D), jnp.float32)
    for shard_index in range(SHARDS):
        partial_value = jnp.dot(y_flat[:, shard_index * block:(shard_index + 1) * block], w_out[layer_index, shard_index * block:(shard_index + 1) * block], preferred_element_type=jnp.float32).astype(jnp.bfloat16)
        summed = summed + lax.optimization_barrier(partial_value).astype(jnp.float32)
    return (h_float + summed.reshape(row_count, LEN, D)).astype(jnp.bfloat16)

def reference(stream, norm_gain, w_x, w_bc, w_dt, conv_x, conv_bc, dt_bias, decay_rate, skip_d, y_gain, w_out):
    current = stream.reshape(MICRO * SEQS, LEN, D)
    outputs = []
    for layer_index in range(LAYERS):
        current = apply_layer(current, layer_index, norm_gain, w_x, w_bc, w_dt, conv_x, conv_bc, dt_bias, decay_rate, skip_d, y_gain, w_out)
        outputs.append(current.reshape(MICRO, SEQS, LEN, D))
    return jnp.stack(outputs, axis=0)
```

```python
import functools

import jax
import jax.numpy as jnp
from jax import lax
from jax.experimental import pallas as pl
from jax.experimental.pallas import tpu as pltpu
from jax.sharding import PartitionSpec as P

MESH = pl.DeviceIdType.MESH
HEAD_DIM = 64
STATE = 128
NX = 4
NY = 4
NZ = 8
MICRO = 2
LEN = 128
ROWS = NX * LEN
WIDTH = 1024
BC = 2 * STATE
COLS = WIDTH + BC + 128
HALF = 64
EPS = 1e-05
F32 = jnp.float32
BF16 = jnp.bfloat16


def remote(src, dst, send_sem, recv_sem, device):
    return pltpu.make_async_remote_copy(
        src_ref=src,
        dst_ref=dst,
        send_sem=send_sem,
        recv_sem=recv_sem,
        device_id=device,
        device_id_type=MESH,
    )


def kernel(
    stream_ref,
    w_in_ref,
    w_out_ref,
    par_ref,
    out_ref,
    staged,
    w_in,
    w_out,
    act,
    scaled,
    part,
    got,
    padded,
    conv,
    y_raw,
    y_all,
    proj,
    proj_got,
    h_next,
    squares,
    in_send,
    in_recv,
    wout_send,
    wout_recv,
    first_send,
    first_recv,
    next_send,
    next_recv,
    part_send,
    part_recv,
    y_send,
    y_recv,
    proj_send,
    proj_recv,
    out_send,
    out_recv,
    go_sem,
):
    section = lax.axis_index("section")
    dp = lax.axis_index("dp")
    y = lax.axis_index("head")
    z = dp // NX
    x = dp % NX

    def at(s, zz, xx, yy):
        return (s, zz * NX + xx, yy)

    right, left = (z + 1) % NZ, (z + NZ - 1) % NZ

    barrier = pltpu.get_barrier_semaphore()
    for dx in range(NX):
        for dy in range(NY):
            if dx or dy:
                pl.semaphore_signal(
                    barrier,
                    inc=1,
                    device_id=at(section, z, (x + dx) % NX, (y + dy) % NY),
                    device_id_type=MESH,
                )
    for dy in range(NY):
        pl.semaphore_signal(
            barrier, inc=1, device_id=at(1 - section, z, x, (y + dy) % NY), device_id_type=MESH
        )
    for zz in (right, left):
        pl.semaphore_signal(
            barrier, inc=1, device_id=at(section, zz, x, y), device_id_type=MESH
        )
    pl.semaphore_wait(barrier, NX * NY - 1 + NY + 2)

    def in_hop(direction, step, half):
        owner = (z + NZ - step) % NZ if direction == 0 else (z + step) % NZ
        rows = (
            pl.ds(pl.multiple_of(owner * LEN, LEN), LEN)
            if not half
            else pl.ds(pl.multiple_of(owner * LEN + direction * HALF, HALF), HALF)
        )
        src = w_in.at[rows]
        return remote(
            src,
            src,
            in_send.at[direction, step],
            in_recv.at[direction, step],
            at(section, right if direction == 0 else left, x, y),
        )

    def out_hop(direction, step, half):
        owner = (z + NZ - step) % NZ if direction == 0 else (z + step) % NZ
        columns = pl.ds(pl.multiple_of(owner * LEN, LEN), LEN)
        src = (
            w_out.at[:, columns]
            if not half
            else w_out.at[pl.ds(direction * (WIDTH // 2), WIDTH // 2), columns]
        )
        return remote(
            src,
            src,
            wout_send.at[direction, step],
            wout_recv.at[direction, step],
            at(section, right if direction == 0 else left, x, y),
        )

    def ring_start(hop):
        for direction in range(2):
            hop(direction, 0, False).start()

    def ring_step(hop, step, last):
        for direction in range(2):
            hop(direction, step - 1, False).wait_recv()
            hop(direction, step, last).start()

    def ring_end(hop):
        for direction in range(2):
            hop(direction, 3, True).wait_recv()

    own_rows = pl.ds(pl.multiple_of(z * LEN, LEN), LEN)
    w_in[own_rows, :] = w_in_ref[...]
    w_out[:, own_rows] = w_out_ref[0]

    @pl.when(section == 1)
    def _():
        pl.semaphore_wait(go_sem, 1)

    ring_start(in_hop)

    def first(m, dx, dy):
        to_x = (x + dx) % NX
        to_y = (y + dy) % NY
        return remote(
            staged.at[m, to_x],
            act.at[m, y, pl.ds(pl.multiple_of(x * LEN, LEN), LEN), :],
            first_send.at[m, dx, dy],
            first_recv.at[m, dx, dy],
            at(0, z, to_x, to_y),
        )

    @pl.when(section == 0)
    def _():
        for m in range(MICRO):
            for xx in range(NX):
                staged[m, xx, :, :LEN] = stream_ref[m, 0, :, xx * LEN : (xx + 1) * LEN]
                staged[m, xx, :, LEN:] = stream_ref[
                    m, 0, :, (xx + NX) * LEN : (xx + NX + 1) * LEN
                ]
            act[m, y, pl.ds(pl.multiple_of(x * LEN, LEN), LEN), :] = staged[m, x]
            for dx in range(NX):
                for dy in range(NY):
                    if dx or dy:
                        first(m, dx, dy).start()

    for step in range(1, 4):
        ring_step(in_hop, step, step == 3)
    ring_end(in_hop)

    @pl.when(section == 0)
    def _():
        pl.semaphore_signal(go_sem, inc=1, device_id=at(1, z, x, y), device_id_type=MESH)

    ring_start(out_hop)

    def onward(m, dy):
        return remote(
            h_next.at[m],
            act.at[m, y],
            next_send.at[m, dy],
            next_recv.at[m, dy],
            at(1 - section, z, x, (y + dy) % NY),
        )

    def send_part(m, dx):
        to_x = (x + dx) % NX
        return remote(
            part.at[m, pl.ds(pl.multiple_of(to_x * LEN, LEN), LEN), :],
            got.at[m, dx],
            part_send.at[m, dx],
            part_recv.at[m, dx],
            at(section, z, to_x, y),
        )

    def send_y(m, dx):
        return remote(
            y_all.at[m, x],
            y_all.at[m, x],
            y_send.at[m, dx],
            y_recv.at[m, dx],
            at(section, z, (x + dx) % NX, y),
        )

    def send_proj(m, dy):
        to_y = (y + dy) % NY
        return remote(
            proj.at[m, to_y],
            proj_got.at[m, dy],
            proj_send.at[m, dy],
            proj_recv.at[m, dy],
            at(section, z, x, to_y),
        )

    def send_out(m, dx, part_of):
        to_x = (x + dx) % NX
        return remote(
            h_next.at[
                m,
                pl.ds(pl.multiple_of(to_x * LEN, LEN), LEN),
                part_of * LEN : (part_of + 1) * LEN,
            ],
            out_ref.at[
                0, m, 0, :, pl.ds(pl.multiple_of((x + NX * part_of) * LEN, LEN), LEN)
            ],
            out_send.at[m, dx, part_of],
            out_recv.at[m, dx, part_of],
            at(section, z, to_x, y),
        )

    lane = lax.broadcasted_iota(jnp.int32, (LEN, LEN), 1)
    row = lax.broadcasted_iota(jnp.int32, (LEN, LEN), 0)

    def project_in(m):
        @pl.when(section == 0)
        def _():
            for dx in range(NX):
                for dy in range(NY):
                    if dx or dy:
                        first(m, dx, dy).wait_recv()

        @pl.when(section == 1)
        def _():
            for dy in range(NY):
                onward(m, dy).wait_recv()

        def scale(i, carry):
            rows = pl.ds(pl.multiple_of(i * 64, 64), 64)
            total = jnp.zeros((64, LEN), F32)
            for yy in range(NY):
                for half in range(2):
                    at_ = yy * 2 * LEN + half * LEN
                    value = act[m, yy, rows, half * LEN : (half + 1) * LEN].astype(F32)
                    total = total + value * value
                    gain = par_ref[8 + x, :, at_ : at_ + LEN]
                    scaled[rows, at_ : at_ + LEN] = (value * gain).astype(BF16)
            squares[rows, :] = jnp.broadcast_to(jnp.sum(total, axis=1, keepdims=True), (64, LEN))
            return carry

        lax.fori_loop(0, ROWS // 64, scale, 0)

        def columns(i, carry):
            cols = pl.ds(pl.multiple_of(i * 256, 256), 256)
            part[m, :, cols] = jnp.dot(
                scaled[...], w_in[:, cols], preferred_element_type=F32
            ).astype(BF16)
            return carry

        lax.fori_loop(0, (WIDTH + BC) // 256, columns, 0)
        small = jnp.dot(scaled[...], w_in[:, WIDTH + BC :], preferred_element_type=F32)
        high = small.astype(BF16).astype(F32)
        low = small - high
        square = squares[...]
        square_high = square.astype(BF16).astype(F32)
        lanes = lax.broadcasted_iota(jnp.int32, (ROWS, LEN), 1)
        packed = high + pltpu.roll(low, 16, 1)
        packed = jnp.where(lanes == 32, square_high, packed)
        packed = jnp.where(lanes == 33, square - square_high, packed)
        part[m, :, WIDTH + BC :] = packed.astype(BF16)
        for dx in (1, 3, 2):
            send_part(m, dx).start()

    def mix(m):
        for dx in (1, 3, 2):
            send_part(m, dx).wait_recv()
        own = pl.ds(pl.multiple_of(x * LEN, LEN), LEN)

        def summed(cols):
            total = part[m, own, cols].astype(F32)
            for dx in (1, 2, 3):
                total = total + got[m, dx, :, cols].astype(F32)
            return total

        tail = summed(slice(WIDTH + BC, COLS))
        square = tail[:, 32:33] + tail[:, 33:34]
        inverse = lax.rsqrt(square * (1.0 / (NX * WIDTH)) + EPS)
        raw = (tail + pltpu.roll(tail, LEN - 16, 1)) * inverse
        pre = raw + par_ref[6, :, :LEN]
        steps = jnp.maximum(pre, 0.0) + jnp.log1p(jnp.exp(-jnp.abs(pre)))
        steps = jnp.where(lane < 16, steps, 0.0)
        lower = jnp.where(row >= lane, 1.0, 0.0)
        decay = jnp.dot(
            lower,
            steps * par_ref[7, :, :LEN],
            precision=lax.Precision.HIGHEST,
            preferred_element_type=F32,
        )
        decay_t = decay.T
        inverse_wide = jnp.broadcast_to(inverse, (LEN, LEN))

        padded[0:8, :] = jnp.zeros((8, LEN), F32)

        for c in range((WIDTH + BC) // LEN):
            cols = slice(c * LEN, (c + 1) * LEN)
            padded[8:, :] = summed(cols) * inverse_wide
            value = jnp.zeros((LEN, LEN), F32)
            for tap in range(4):
                value = value + par_ref[tap, :, cols] * padded[5 + tap : 5 + tap + LEN, :]
            conv[:, cols] = value / (1.0 + jnp.exp(-value))

        scores = lax.dot_general(
            conv[:, WIDTH + STATE : WIDTH + BC],
            conv[:, WIDTH : WIDTH + STATE],
            (((1,), (1,)), ((), ())),
            precision=lax.Precision.HIGHEST,
            preferred_element_type=F32,
        )
        scores = jnp.where(row >= lane, scores, 0.0)
        power = jnp.zeros((LEN, LEN), F32)
        for pair in range(WIDTH // LEN):
            cols = slice(pair * LEN, (pair + 1) * LEN)
            mixes = []
            for j in (2 * pair, 2 * pair + 1):
                gap = jnp.minimum(decay_t[j : j + 1, :] - decay[:, j : j + 1], 0.0)
                mixes.append((jnp.exp(gap) * scores).astype(BF16))
            value = conv[:, cols]
            step = jnp.where(
                lane < HEAD_DIM,
                steps[:, 2 * pair : 2 * pair + 1],
                steps[:, 2 * pair + 1 : 2 * pair + 2],
            )
            stepped = value * step
            blocks = jnp.concatenate(
                [
                    jnp.where(lane < HEAD_DIM, stepped, 0.0).astype(BF16),
                    jnp.where(lane < HEAD_DIM, 0.0, stepped).astype(BF16),
                ],
                axis=0,
            )
            mixed = jnp.dot(
                jnp.concatenate(mixes, axis=1), blocks, preferred_element_type=F32
            )
            mixed = mixed + par_ref[5, :, cols] * value
            power = power + mixed * mixed
            y_raw[:, cols] = mixed
        norm = lax.rsqrt(jnp.sum(power, axis=1, keepdims=True) * (1.0 / WIDTH) + EPS)
        norm = jnp.broadcast_to(norm, (LEN, LEN))
        for c in range(WIDTH // LEN):
            cols = slice(c * LEN, (c + 1) * LEN)
            y_all[m, x, :, cols] = (y_raw[:, cols] * norm * par_ref[4, :, cols]).astype(BF16)
        for dx in (1, 3, 2):
            send_y(m, dx).start()

    def project_out(m):
        for dx in (1, 3, 2):
            send_y(m, dx).wait_recv()

        values = y_all[m].reshape(ROWS, WIDTH)
        for dy in (1, 3, 2, 0):
            to_y = (y + dy) % NY
            cols = pl.ds(pl.multiple_of(to_y * 2 * LEN, 2 * LEN), 2 * LEN)
            proj[m, to_y] = jnp.dot(
                values, w_out[:, cols], preferred_element_type=F32
            ).astype(BF16)
            if dy:
                send_proj(m, dy).start()

    def finish(m):
        for dy in (1, 3, 2):
            send_proj(m, dy).wait_recv()

        def add(i, carry):
            rows = pl.ds(pl.multiple_of(i * 64, 64), 64)
            total = proj[m, y, rows, :].astype(F32)
            for dy in (1, 2, 3):
                total = total + proj_got[m, dy, rows, :].astype(F32)
            h_next[m, rows, :] = (act[m, y, rows, :].astype(F32) + total).astype(BF16)
            return carry

        lax.fori_loop(0, ROWS // 64, add, 0)

        @pl.when(section == 0)
        def _():
            for dy in (1, 3, 2, 0):
                onward(m, dy).start()

        for dx in (1, 3, 2):
            for part_of in range(2):
                send_out(m, dx, part_of).start()
        own = pl.ds(pl.multiple_of(x * LEN, LEN), LEN)
        for part_of in range(2):
            out_ref[
                0, m, 0, :, pl.ds(pl.multiple_of((x + NX * part_of) * LEN, LEN), LEN)
            ] = h_next[m, own, part_of * LEN : (part_of + 1) * LEN]

    def stage_in(m, carry):
        project_in(m)
        ring_step(out_hop, m + 1, False)
        return carry

    def stage_mix(m, carry):
        mix(m)
        return carry

    def stage_out(m, carry):
        project_out(m)
        return carry

    def stage_end(m, carry):
        finish(m)
        return carry

    lax.fori_loop(0, MICRO, stage_in, 0)
    ring_step(out_hop, 3, True)
    lax.fori_loop(0, MICRO, stage_mix, 0)
    ring_end(out_hop)
    lax.fori_loop(0, MICRO, stage_out, 0)
    lax.fori_loop(0, MICRO, stage_end, 0)

    def drain(m, carry):
        for dx in (1, 2, 3):
            for part_of in range(2):
                send_out(m, dx, part_of).wait()
            send_part(m, dx).wait_send()
            send_y(m, dx).wait_send()
        for dy in (1, 2, 3):
            send_proj(m, dy).wait_send()

        @pl.when(section == 0)
        def _():
            for dy in range(NY):
                onward(m, dy).wait_send()
            for dx in range(NX):
                for dy in range(NY):
                    if dx or dy:
                        first(m, dx, dy).wait_send()

        return carry

    lax.fori_loop(0, MICRO, drain, 0)
    for step in range(4):
        for direction in range(2):
            in_hop(direction, step, step == 3).wait_send()
            out_hop(direction, step, step == 3).wait_send()


def body(
    stream, norm_gain, w_x, w_bc, w_dt, conv_x, conv_bc, dt_bias, decay_rate, skip_d, y_gain, w_out
):
    w_in = jnp.concatenate(
        [w_x[0], w_bc[0], jnp.pad(w_dt[0], ((0, 0), (0, 128 - w_dt.shape[2])))], axis=1
    )

    def wide(rows):
        return jnp.pad(rows, ((0, 0), (0, COLS - rows.shape[1])))

    gains = norm_gain[0].reshape(NZ, NX, LEN).transpose(1, 0, 2).reshape(NX, WIDTH)
    params = jnp.concatenate(
        [
            wide(jnp.concatenate([conv_x[0], conv_bc[0]], axis=1)),
            wide(y_gain),
            wide(jnp.repeat(skip_d, HEAD_DIM, axis=1)),
            wide(dt_bias),
            wide(decay_rate),
            wide(gains),
        ],
        axis=0,
    ).reshape(8 + NX, 1, COLS)
    vmem = pl.BlockSpec(memory_space=pltpu.VMEM)
    dma = pltpu.SemaphoreType.DMA
    return pl.pallas_call(
        kernel,
        out_shape=jax.ShapeDtypeStruct((1, MICRO, 1, LEN, WIDTH), BF16),
        in_specs=[vmem] * 4,
        out_specs=vmem,
        scratch_shapes=[
            pltpu.VMEM((MICRO, NX, LEN, 2 * LEN), BF16),
            pltpu.VMEM((NZ * LEN, COLS), BF16),
            pltpu.VMEM((WIDTH, NZ * LEN), BF16),
            pltpu.VMEM((MICRO, NY, ROWS, 2 * LEN), BF16),
            pltpu.VMEM((ROWS, WIDTH), BF16),
            pltpu.VMEM((MICRO, ROWS, COLS), BF16),
            pltpu.VMEM((MICRO, NX, LEN, COLS), BF16),
            pltpu.VMEM((8 + LEN, LEN), F32),
            pltpu.VMEM((LEN, WIDTH + BC), F32),
            pltpu.VMEM((LEN, WIDTH), F32),
            pltpu.VMEM((MICRO, NX, LEN, WIDTH), BF16),
            pltpu.VMEM((MICRO, NY, ROWS, 2 * LEN), BF16),
            pltpu.VMEM((MICRO, NY, ROWS, 2 * LEN), BF16),
            pltpu.VMEM((MICRO, ROWS, 2 * LEN), BF16),
            pltpu.VMEM((ROWS, LEN), F32),
            dma((2, 4)),
            dma((2, 4)),
            dma((2, 4)),
            dma((2, 4)),
            dma((MICRO, NX, NY)),
            dma((MICRO, NX, NY)),
            dma((MICRO, NY)),
            dma((MICRO, NY)),
            dma((MICRO, NX)),
            dma((MICRO, NX)),
            dma((MICRO, NX)),
            dma((MICRO, NX)),
            dma((MICRO, NY)),
            dma((MICRO, NY)),
            dma((MICRO, NX, 2)),
            dma((MICRO, NX, 2)),
            pltpu.SemaphoreType.REGULAR,
        ],
        compiler_params=pltpu.CompilerParams(
            collective_id=0, has_side_effects=True, vmem_limit_bytes=48 * 1024 * 1024
        ),
        name="mixer",
    )(stream, w_in, w_out, params)


def solution(mesh):
    in_specs = (
        P(None, "dp", None, "head"),
        P("section", None),
        P("section", "dp", "head"),
        P("section", "dp", "head"),
        P("section", "dp", "head"),
        P("section", None, "head"),
        P("section", None, "head"),
        P("section", "head"),
        P("section", "head"),
        P("section", "head"),
        P("section", "head"),
        P("section", "head", "dp"),
    )
    out_specs = P("section", None, "dp", None, "head")
    return jax.shard_map(body, mesh=mesh, in_specs=in_specs, out_specs=out_specs, check_vma=False)
```

```python
import functools

import jax
import jax.numpy as jnp
from jax import lax
from jax.experimental import pallas as pl
from jax.experimental.pallas import tpu as pltpu
from jax.sharding import PartitionSpec as P

MESH = pl.DeviceIdType.MESH
HEAD_DIM = 64
STATE = 128
NX = 4
NY = 4
NZ = 8
MICRO = 2
LEN = 128
ROWS = NX * LEN
WIDTH = 1024
BC = 2 * STATE
COLS = WIDTH + BC + 128
CHUNKS = 4
EPS = 1e-05
F32 = jnp.float32
BF16 = jnp.bfloat16


def remote(src, dst, send_sem, recv_sem, device):
    return pltpu.make_async_remote_copy(
        src_ref=src,
        dst_ref=dst,
        send_sem=send_sem,
        recv_sem=recv_sem,
        device_id=device,
        device_id_type=MESH,
    )


def kernel(
    stream_ref,
    gain_ref,
    w_x_ref,
    w_bc_ref,
    w_dt_ref,
    conv_x_ref,
    conv_bc_ref,
    bias_ref,
    rate_ref,
    skip_ref,
    y_gain_ref,
    w_out_ref,
    out_ref,
    staged,
    gains,
    w_dt,
    taps,
    biases,
    rates,
    skips,
    y_gains,
    w_in,
    w_out,
    relay,
    act,
    scaled,
    part,
    got,
    padded,
    conv,
    y_raw,
    y_all,
    proj,
    proj_got,
    h_next,
    squares,
    in_send,
    in_recv,
    wout_send,
    wout_recv,
    first_send,
    first_recv,
    next_send,
    next_recv,
    part_send,
    part_recv,
    y_send,
    y_recv,
    proj_send,
    proj_recv,
    out_send,
    out_recv,
    relay_send,
    relay_recv,
    push_send,
    push_recv,
    own_send,
    own_recv,
    load_sem,
    stream_sem,
    go_sem,
):
    section = lax.axis_index("section")
    dp = lax.axis_index("dp")
    y = lax.axis_index("head")
    z = dp // NX
    x = dp % NX

    def at(s, zz, xx, yy):
        return (s, zz * NX + xx, yy)

    right, left = (z + 1) % NZ, (z + NZ - 1) % NZ
    sibling = at(1 - section, z, x, y)
    own_block = pl.ds(pl.multiple_of(z * LEN, LEN), LEN)

    loads = [
        pltpu.make_async_copy(source, target, load_sem.at[i])
        for i, (source, target) in enumerate(
            [
                (w_out_ref.at[0], w_out.at[:, own_block]),
                (w_x_ref.at[0], w_in.at[own_block, :WIDTH]),
                (w_bc_ref.at[0], w_in.at[own_block, WIDTH : WIDTH + BC]),
                (w_dt_ref.at[0], w_dt),
                (gain_ref, gains),
                (conv_x_ref.at[0], taps.at[:, :WIDTH]),
                (conv_bc_ref.at[0], taps.at[:, WIDTH:]),
                (bias_ref, biases),
                (rate_ref, rates),
                (skip_ref, skips),
                (y_gain_ref, y_gains),
            ]
        )
    ]
    for load in loads:
        load.start()

    def stage(m, xx, half):
        return pltpu.make_async_copy(
            stream_ref.at[m, 0, :, pl.ds((xx + NX * half) * LEN, LEN)],
            staged.at[m, xx, :, pl.ds(half * LEN, LEN)],
            stream_sem.at[m, xx, half],
        )

    @pl.when(section == 0)
    def _():
        for m in range(MICRO):
            for xx in range(NX):
                for half in range(2):
                    stage(m, xx, half).start()

    barrier = pltpu.get_barrier_semaphore()
    for dx in range(NX):
        for dy in range(NY):
            if dx or dy:
                pl.semaphore_signal(
                    barrier,
                    inc=1,
                    device_id=at(section, z, (x + dx) % NX, (y + dy) % NY),
                    device_id_type=MESH,
                )
    for dy in range(NY):
        pl.semaphore_signal(
            barrier, inc=1, device_id=at(1 - section, z, x, (y + dy) % NY), device_id_type=MESH
        )
    for zz in (right, left):
        pl.semaphore_signal(
            barrier, inc=1, device_id=at(section, zz, x, y), device_id_type=MESH
        )
    pl.semaphore_wait(barrier, NX * NY - 1 + NY + 2)

    def hop(buffer, by_rows, sends, receives):
        def one(direction, step, chunk):
            owner = (z + NZ - step) % NZ if direction == 0 else (z + step) % NZ
            if by_rows:
                size = LEN // CHUNKS
                piece = buffer.at[pl.ds(pl.multiple_of(owner * LEN + chunk * size, size), size)]
            else:
                size = WIDTH // CHUNKS
                piece = buffer.at[
                    pl.ds(chunk * size, size), pl.ds(pl.multiple_of(owner * LEN, LEN), LEN)
                ]
            return remote(
                piece,
                piece,
                sends.at[direction, step, chunk],
                receives.at[direction, step, chunk],
                at(section, right if direction == 0 else left, x, y),
            )

        return one

    in_hop = hop(w_in, True, in_send, in_recv)
    out_hop = hop(w_out, False, wout_send, wout_recv)
    relay_hop = hop(relay, False, relay_send, relay_recv)

    def pieces(step):
        half = CHUNKS // 2
        return [
            (chunk, direction)
            for chunk in range(CHUNKS)
            for direction in range(2)
            if step < 3 or chunk // half == direction
        ]

    def ring_start(one):
        for chunk, direction in pieces(0):
            one(direction, 0, chunk).start()

    def ring_middle(one, arrived=None):
        for step in range(1, 4):
            for chunk, direction in pieces(0):
                one(direction, step - 1, chunk).wait_recv()
                if (chunk, direction) in pieces(step):
                    one(direction, step, chunk).start()
            if arrived is not None:
                arrived(step)

    def ring_end(one):
        for chunk, direction in pieces(3):
            one(direction, 3, chunk).wait_recv()

    def ring_drain(one):
        for step in range(4):
            for chunk, direction in pieces(step):
                one(direction, step, chunk).wait_send()

    def own_out():
        return remote(
            w_out.at[:, own_block], relay.at[:, own_block], own_send, own_recv, sibling
        )

    def push(step):
        columns = pl.ds(pl.multiple_of((z + step) % NZ * LEN, LEN), LEN)
        return remote(
            relay.at[:, columns],
            w_out.at[:, columns],
            push_send.at[step],
            push_recv.at[step],
            sibling,
        )

    def push_both(step):
        push(step).start()
        push(NZ - step).start()

    loads[0].wait()

    @pl.when(section == 0)
    def _():
        own_out().start()

    for load in loads[1:]:
        load.wait()
    w_in[own_block, WIDTH + BC :] = jnp.concatenate(
        [w_dt[...], jnp.zeros((LEN, LEN - 16), BF16)], axis=1
    )

    def first(m, dx, dy):
        to_x = (x + dx) % NX
        to_y = (y + dy) % NY
        return remote(
            staged.at[m, to_x],
            act.at[m, y, pl.ds(pl.multiple_of(x * LEN, LEN), LEN), :],
            first_send.at[m, dx, dy],
            first_recv.at[m, dx, dy],
            at(0, z, to_x, to_y),
        )

    @pl.when(section == 0)
    def _():
        ring_start(in_hop)
        for m in range(MICRO):
            for xx in range(NX):
                for half in range(2):
                    stage(m, xx, half).wait()
            act[m, y, pl.ds(pl.multiple_of(x * LEN, LEN), LEN), :] = staged[m, x]
            for dx in range(NX):
                for dy in range(NY):
                    if dx or dy:
                        first(m, dx, dy).start()
        ring_middle(in_hop)
        pl.semaphore_signal(go_sem, inc=1, device_id=sibling, device_id_type=MESH)

    @pl.when(section == 1)
    def _():
        own_out().wait_recv()
        pl.semaphore_wait(go_sem, 1)
        ring_start(relay_hop)
        ring_middle(relay_hop, push_both)
        ring_start(in_hop)
        ring_end(relay_hop)
        push(NZ // 2).start()
        ring_middle(in_hop)
        ring_start(out_hop)
        ring_end(in_hop)
        ring_middle(out_hop)
        ring_end(out_hop)

    def block(ahead):
        return pl.ds(pl.multiple_of((x + ahead) % NX * LEN, LEN), LEN)

    def order(i):
        return i + i // 2 - i // 3 * 2

    def onward(m, ahead, dy):
        return remote(
            h_next.at[m, block(ahead), :],
            act.at[m, y, block(ahead), :],
            next_send.at[m, ahead, dy],
            next_recv.at[m, ahead, dy],
            at(1 - section, z, x, (y + dy) % NY),
        )

    def send_part(m, ahead):
        return remote(
            part.at[m, block(ahead), :],
            got.at[m, ahead],
            part_send.at[m, ahead],
            part_recv.at[m, ahead],
            at(section, z, (x + ahead) % NX, y),
        )

    def send_y(m, ahead):
        return remote(
            y_all.at[m, x],
            y_all.at[m, x],
            y_send.at[m, ahead],
            y_recv.at[m, ahead],
            at(section, z, (x + ahead) % NX, y),
        )

    def send_proj(m, ahead, dy):
        to_y = (y + dy) % NY
        return remote(
            proj.at[m, to_y, block(ahead), :],
            proj_got.at[m, dy, block(ahead), :],
            proj_send.at[m, ahead, dy],
            proj_recv.at[m, ahead, dy],
            at(section, z, x, to_y),
        )

    def send_out(m, ahead, half):
        return remote(
            h_next.at[m, block(ahead), pl.ds(half * LEN, LEN)],
            out_ref.at[0, m, 0, :, pl.ds(pl.multiple_of((x + NX * half) * LEN, LEN), LEN)],
            out_send.at[m, ahead, half],
            out_recv.at[m, ahead, half],
            at(section, z, (x + ahead) % NX, y),
        )

    lane = lax.broadcasted_iota(jnp.int32, (LEN, LEN), 1)
    row = lax.broadcasted_iota(jnp.int32, (LEN, LEN), 0)

    def prepare(m, ahead):
        def scale(i, carry):
            rows = pl.ds(pl.multiple_of((x + ahead) % NX * LEN + i * 64, 64), 64)
            total = jnp.zeros((64, LEN), F32)
            for yy in range(NY):
                for half in range(2):
                    at_ = yy * 2 * LEN + half * LEN
                    value = act[m, yy, rows, half * LEN : (half + 1) * LEN].astype(F32)
                    total = total + value * value
                    gain = gains[
                        :, pl.ds(pl.multiple_of((yy * 2 + half) * NX * LEN + x * LEN, LEN), LEN)
                    ]
                    scaled[m, rows, at_ : at_ + LEN] = (value * gain).astype(BF16)
            squares[m, rows, :] = jnp.broadcast_to(
                jnp.sum(total, axis=1, keepdims=True), (64, LEN)
            )
            return carry

        lax.fori_loop(0, LEN // 64, scale, 0)

    def project_in(m, ahead):
        rows = block(ahead)
        values = scaled[m, rows, :]
        for c in range((WIDTH + BC) // 256):
            cols = slice(c * 256, (c + 1) * 256)
            part[m, rows, cols] = jnp.dot(
                values, w_in[:, cols], preferred_element_type=F32
            ).astype(BF16)
        small = jnp.dot(values, w_in[:, WIDTH + BC :], preferred_element_type=F32)
        high = small.astype(BF16).astype(F32)
        low = small - high
        square = squares[m, rows, :]
        square_high = square.astype(BF16).astype(F32)
        packed = high + pltpu.roll(low, 16, 1)
        packed = jnp.where(lane == 32, square_high, packed)
        packed = jnp.where(lane == 33, square - square_high, packed)
        part[m, rows, WIDTH + BC :] = packed.astype(BF16)

        @pl.when(ahead != 0)
        def _():
            send_part(m, ahead).start()

    def mix(m):
        for ahead in (1, 3, 2):
            send_part(m, ahead).wait_recv()
        own = block(0)

        def summed(cols):
            total = part[m, own, cols].astype(F32)
            for dx in (1, 2, 3):
                total = total + got[m, dx, :, cols].astype(F32)
            return total

        tail = summed(slice(WIDTH + BC, COLS))
        square = tail[:, 32:33] + tail[:, 33:34]
        inverse = lax.rsqrt(square * (1.0 / (NX * WIDTH)) + EPS)
        raw = (tail + pltpu.roll(tail, LEN - 16, 1)) * inverse
        pre = raw + jnp.concatenate([biases[...], jnp.zeros((1, LEN - 16), F32)], axis=1)
        steps = jnp.maximum(pre, 0.0) + jnp.log1p(jnp.exp(-jnp.abs(pre)))
        steps = jnp.where(lane < 16, steps, 0.0)
        lower = jnp.where(row >= lane, 1.0, 0.0)
        decay = jnp.dot(
            lower,
            steps * jnp.concatenate([rates[...], jnp.zeros((1, LEN - 16), F32)], axis=1),
            precision=lax.Precision.HIGHEST,
            preferred_element_type=F32,
        )
        decay_t = decay.T
        inverse_wide = jnp.broadcast_to(inverse, (LEN, LEN))

        padded[0:8, :] = jnp.zeros((8, LEN), F32)

        for c in range((WIDTH + BC) // LEN):
            cols = slice(c * LEN, (c + 1) * LEN)
            padded[8:, :] = summed(cols) * inverse_wide
            value = jnp.zeros((LEN, LEN), F32)
            for tap in range(4):
                value = value + taps[tap : tap + 1, cols] * padded[5 + tap : 5 + tap + LEN, :]
            conv[:, cols] = value / (1.0 + jnp.exp(-value))

        scores = lax.dot_general(
            conv[:, WIDTH + STATE : WIDTH + BC],
            conv[:, WIDTH : WIDTH + STATE],
            (((1,), (1,)), ((), ())),
            precision=lax.Precision.HIGHEST,
            preferred_element_type=F32,
        )
        scores = jnp.where(row >= lane, scores, 0.0)
        power = jnp.zeros((LEN, LEN), F32)
        for pair in range(WIDTH // LEN):
            cols = slice(pair * LEN, (pair + 1) * LEN)
            mixes = []
            for j in (2 * pair, 2 * pair + 1):
                gap = jnp.minimum(decay_t[j : j + 1, :] - decay[:, j : j + 1], 0.0)
                mixes.append((jnp.exp(gap) * scores).astype(BF16))
            value = conv[:, cols]
            step = jnp.where(
                lane < HEAD_DIM,
                steps[:, 2 * pair : 2 * pair + 1],
                steps[:, 2 * pair + 1 : 2 * pair + 2],
            )
            stepped = value * step
            blocks = jnp.concatenate(
                [
                    jnp.where(lane < HEAD_DIM, stepped, 0.0).astype(BF16),
                    jnp.where(lane < HEAD_DIM, 0.0, stepped).astype(BF16),
                ],
                axis=0,
            )
            mixed = jnp.dot(
                jnp.concatenate(mixes, axis=1), blocks, preferred_element_type=F32
            )
            skip = jnp.where(
                lane[:1] < HEAD_DIM,
                skips[:, 2 * pair : 2 * pair + 1],
                skips[:, 2 * pair + 1 : 2 * pair + 2],
            )
            mixed = mixed + skip * value
            power = power + mixed * mixed
            y_raw[:, cols] = mixed
        norm = lax.rsqrt(jnp.sum(power, axis=1, keepdims=True) * (1.0 / WIDTH) + EPS)
        norm = jnp.broadcast_to(norm, (LEN, LEN))
        for c in range(WIDTH // LEN):
            cols = slice(c * LEN, (c + 1) * LEN)
            y_all[m, x, :, cols] = (y_raw[:, cols] * norm * y_gains[:, cols]).astype(BF16)
        for ahead in (1, 3, 2):
            send_y(m, ahead).start()

    def project_out(m, ahead):
        values = y_all[m, (x + ahead) % NX]
        for dy in (1, 3, 2, 0):
            to_y = (y + dy) % NY
            cols = pl.ds(pl.multiple_of(to_y * 2 * LEN, 2 * LEN), 2 * LEN)
            proj[m, to_y, block(ahead), :] = jnp.dot(
                values, w_out[:, cols], preferred_element_type=F32
            ).astype(BF16)
            if dy:
                send_proj(m, ahead, dy).start()

    def finish(m, ahead):
        for dy in (1, 3, 2):
            send_proj(m, ahead, dy).wait_recv()
        rows = block(ahead)
        total = proj[m, y, rows, :].astype(F32)
        for dy in (1, 2, 3):
            total = total + proj_got[m, dy, rows, :].astype(F32)
        h_next[m, rows, :] = (act[m, y, rows, :].astype(F32) + total).astype(BF16)

        @pl.when(section == 0)
        def _():
            for dy in (1, 3, 2, 0):
                onward(m, ahead, dy).start()

        @pl.when(ahead != 0)
        def _():
            for half in range(2):
                send_out(m, ahead, half).start()

        @pl.when(ahead == 0)
        def _():
            for half in range(2):
                out_ref[
                    0, m, 0, :, pl.ds(pl.multiple_of((x + NX * half) * LEN, LEN), LEN)
                ] = h_next[m, rows, half * LEN : (half + 1) * LEN]

    @pl.when(section == 0)
    def _():
        for m in range(MICRO):
            for dx in range(NX):
                for dy in range(NY):
                    if dx or dy:
                        first(m, dx, dy).wait_recv()

        def all_rows(i, carry):
            prepare(i // NX, i % NX)
            return carry

        lax.fori_loop(0, MICRO * NX, all_rows, 0)
        ring_end(in_hop)

    def stage_in(i, carry):
        m = i // NX
        ahead = order((i + 1 - section) % NX)

        @pl.when(section == 1)
        def _():
            for dy in range(NY):
                onward(m, ahead, dy).wait_recv()
            prepare(m, ahead)

        project_in(m, ahead)
        return carry

    lax.fori_loop(0, MICRO * NX, stage_in, 0)

    @pl.when(section == 0)
    def _():
        for step in range(1, NZ):
            push(step).wait_recv()

    def stage_mix(m, carry):
        mix(m)
        project_out(m, 0)
        finish(m, 0)
        return carry

    lax.fori_loop(0, MICRO, stage_mix, 0)

    def stage_out(i, carry):
        @pl.when(i < MICRO * (NX - 1))
        def _():
            m = i // (NX - 1)
            ahead = order(i % (NX - 1) + 1)
            send_y(m, (NX - ahead) % NX).wait_recv()
            project_out(m, ahead)

        @pl.when(i > 0)
        def _():
            finish((i - 1) // (NX - 1), order((i - 1) % (NX - 1) + 1))

        return carry

    lax.fori_loop(0, MICRO * (NX - 1) + 1, stage_out, 0)

    def drain(m, carry):
        for ahead in (1, 2, 3):
            for half in range(2):
                send_out(m, ahead, half).wait()
            send_part(m, ahead).wait_send()
            send_y(m, ahead).wait_send()
        for ahead in range(NX):
            for dy in (1, 2, 3):
                send_proj(m, ahead, dy).wait_send()

        @pl.when(section == 0)
        def _():
            for ahead in range(NX):
                for dy in range(NY):
                    onward(m, ahead, dy).wait_send()
                    if ahead or dy:
                        first(m, ahead, dy).wait_send()

        return carry

    lax.fori_loop(0, MICRO, drain, 0)
    ring_drain(in_hop)

    @pl.when(section == 0)
    def _():
        own_out().wait_send()

    @pl.when(section == 1)
    def _():
        ring_drain(relay_hop)
        ring_drain(out_hop)
        for step in range(1, NZ):
            push(step).wait_send()


def body(
    stream, norm_gain, w_x, w_bc, w_dt, conv_x, conv_bc, dt_bias, decay_rate, skip_d, y_gain, w_out
):
    vmem = pl.BlockSpec(memory_space=pltpu.VMEM)
    whole = pl.BlockSpec(memory_space=pltpu.HBM)
    dma = pltpu.SemaphoreType.DMA
    return pl.pallas_call(
        kernel,
        out_shape=jax.ShapeDtypeStruct((1, MICRO, 1, LEN, WIDTH), BF16),
        in_specs=[whole] * 12,
        out_specs=vmem,
        scratch_shapes=[
            pltpu.VMEM((MICRO, NX, LEN, 2 * LEN), BF16),
            pltpu.VMEM((1, NX * WIDTH), F32),
            pltpu.VMEM((LEN, 16), BF16),
            pltpu.VMEM((4, WIDTH + BC), F32),
            pltpu.VMEM((1, 16), F32),
            pltpu.VMEM((1, 16), F32),
            pltpu.VMEM((1, 16), F32),
            pltpu.VMEM((1, WIDTH), F32),
            pltpu.VMEM((NZ * LEN, COLS), BF16),
            pltpu.VMEM((WIDTH, NZ * LEN), BF16),
            pltpu.VMEM((WIDTH, NZ * LEN), BF16),
            pltpu.VMEM((MICRO, NY, ROWS, 2 * LEN), BF16),
            pltpu.VMEM((MICRO, ROWS, WIDTH), BF16),
            pltpu.VMEM((MICRO, ROWS, COLS), BF16),
            pltpu.VMEM((MICRO, NX, LEN, COLS), BF16),
            pltpu.VMEM((8 + LEN, LEN), F32),
            pltpu.VMEM((LEN, WIDTH + BC), F32),
            pltpu.VMEM((LEN, WIDTH), F32),
            pltpu.VMEM((MICRO, NX, LEN, WIDTH), BF16),
            pltpu.VMEM((MICRO, NY, ROWS, 2 * LEN), BF16),
            pltpu.VMEM((MICRO, NY, ROWS, 2 * LEN), BF16),
            pltpu.VMEM((MICRO, ROWS, 2 * LEN), BF16),
            pltpu.VMEM((MICRO, ROWS, LEN), F32),
            dma((2, 4, CHUNKS)),
            dma((2, 4, CHUNKS)),
            dma((2, 4, CHUNKS)),
            dma((2, 4, CHUNKS)),
            dma((MICRO, NX, NY)),
            dma((MICRO, NX, NY)),
            dma((MICRO, NX, NY)),
            dma((MICRO, NX, NY)),
            dma((MICRO, NX)),
            dma((MICRO, NX)),
            dma((MICRO, NX)),
            dma((MICRO, NX)),
            dma((MICRO, NX, NY)),
            dma((MICRO, NX, NY)),
            dma((MICRO, NX, 2)),
            dma((MICRO, NX, 2)),
            dma((2, 4, CHUNKS)),
            dma((2, 4, CHUNKS)),
            dma((NZ,)),
            dma((NZ,)),
            dma,
            dma,
            dma((11,)),
            dma((MICRO, NX, 2)),
            pltpu.SemaphoreType.REGULAR,
        ],
        compiler_params=pltpu.CompilerParams(
            collective_id=0, has_side_effects=True, vmem_limit_bytes=60 * 1024 * 1024
        ),
        name="mixer",
    )(
        stream,
        norm_gain,
        w_x,
        w_bc,
        w_dt,
        conv_x,
        conv_bc,
        dt_bias,
        decay_rate,
        skip_d,
        y_gain,
        w_out,
    )


def solution(mesh):
    in_specs = (
        P(None, "dp", None, "head"),
        P("section", None),
        P("section", "dp", "head"),
        P("section", "dp", "head"),
        P("section", "dp", "head"),
        P("section", None, "head"),
        P("section", None, "head"),
        P("section", "head"),
        P("section", "head"),
        P("section", "head"),
        P("section", "head"),
        P("section", "head", "dp"),
    )
    out_specs = P("section", None, "dp", None, "head")
    return jax.shard_map(body, mesh=mesh, in_specs=in_specs, out_specs=out_specs, check_vma=False)
```

```python
import functools

import jax
import jax.numpy as jnp
from jax import lax
from jax.experimental import pallas as pl
from jax.experimental.pallas import tpu as pltpu
from jax.sharding import PartitionSpec as P

MESH = pl.DeviceIdType.MESH
HEAD_DIM = 64
STATE = 128
NX = 4
NY = 4
NZ = 8
MICRO = 2
LEN = 128
ROWS = NX * LEN
WIDTH = 1024
BC = 2 * STATE
COLS = WIDTH + BC + 128
CHUNKS = 4
HALF = LEN // 2
EPS = 1e-05
F32 = jnp.float32
BF16 = jnp.bfloat16


def remote(src, dst, send_sem, recv_sem, device):
    return pltpu.make_async_remote_copy(
        src_ref=src,
        dst_ref=dst,
        send_sem=send_sem,
        recv_sem=recv_sem,
        device_id=device,
        device_id_type=MESH,
    )


def kernel(
    stream_ref,
    gain_ref,
    w_x_ref,
    w_bc_ref,
    w_dt_ref,
    conv_x_ref,
    conv_bc_ref,
    bias_ref,
    rate_ref,
    skip_ref,
    y_gain_ref,
    w_out_ref,
    out_ref,
    staged,
    gains,
    taps,
    biases,
    rates,
    skips,
    y_gains,
    w_in,
    w_out,
    relay,
    w_step,
    act,
    scaled,
    part,
    got,
    hop_got,
    padded,
    conv,
    y_raw,
    y_all,
    proj,
    proj_got,
    h_next,
    squares,
    in_send,
    in_recv,
    step_send,
    step_recv,
    wout_send,
    wout_recv,
    first_send,
    first_recv,
    next_send,
    next_recv,
    hop_send,
    hop_recv,
    part_send,
    part_recv,
    y_send,
    y_recv,
    pass_send,
    pass_recv,
    proj_send,
    proj_recv,
    out_send,
    out_recv,
    relay_send,
    relay_recv,
    push_send,
    push_recv,
    own_send,
    own_recv,
    load_sem,
    stream_sem,
    go_sem,
):
    section = lax.axis_index("section")
    dp = lax.axis_index("dp")
    y = lax.axis_index("head")
    z = dp // NX
    x = dp % NX

    def at(s, zz, xx, yy):
        return (s, zz * NX + xx, yy)

    right, left = (z + 1) % NZ, (z + NZ - 1) % NZ
    sibling = at(1 - section, z, x, y)
    own_block = pl.ds(pl.multiple_of(z * LEN, LEN), LEN)

    loads = [
        pltpu.make_async_copy(source, target, load_sem.at[i])
        for i, (source, target) in enumerate(
            [
                (w_out_ref.at[0], w_out.at[:, own_block]),
                (w_x_ref.at[0], w_in.at[own_block, :WIDTH]),
                (w_bc_ref.at[0], w_in.at[own_block, WIDTH : WIDTH + BC]),
                (w_dt_ref.at[0], w_step.at[:16, own_block]),
                (gain_ref, gains),
                (conv_x_ref.at[0], taps.at[:, :WIDTH]),
                (conv_bc_ref.at[0], taps.at[:, WIDTH:]),
                (bias_ref, biases),
                (rate_ref, rates),
                (skip_ref, skips),
                (y_gain_ref, y_gains),
            ]
        )
    ]
    for load in loads:
        load.start()

    def stage(m, xx, half):
        return pltpu.make_async_copy(
            stream_ref.at[m, 0, :, pl.ds((xx + NX * half) * LEN, LEN)],
            staged.at[m, xx, :, pl.ds(half * LEN, LEN)],
            stream_sem.at[m, xx, half],
        )

    @pl.when(section == 0)
    def _():
        for m in range(MICRO):
            for xx in range(NX):
                for half in range(2):
                    stage(m, xx, half).start()

    barrier = pltpu.get_barrier_semaphore()
    for dx in range(NX):
        for dy in range(NY):
            if dx or dy:
                pl.semaphore_signal(
                    barrier,
                    inc=1,
                    device_id=at(section, z, (x + dx) % NX, (y + dy) % NY),
                    device_id_type=MESH,
                )
    for dy in range(NY):
        pl.semaphore_signal(
            barrier, inc=1, device_id=at(1 - section, z, x, (y + dy) % NY), device_id_type=MESH
        )
    for zz in (right, left):
        pl.semaphore_signal(
            barrier, inc=1, device_id=at(section, zz, x, y), device_id_type=MESH
        )
    pl.semaphore_wait(barrier, NX * NY - 1 + NY + 2)

    def hop(buffer, by_rows, sends, receives):
        def one(direction, step, chunk):
            owner = (z + NZ - step) % NZ if direction == 0 else (z + step) % NZ
            if by_rows:
                size = LEN // CHUNKS
                piece = buffer.at[pl.ds(pl.multiple_of(owner * LEN + chunk * size, size), size)]
            else:
                size = WIDTH // CHUNKS
                piece = buffer.at[
                    pl.ds(chunk * size, size), pl.ds(pl.multiple_of(owner * LEN, LEN), LEN)
                ]
            return remote(
                piece,
                piece,
                sends.at[direction, step, chunk],
                receives.at[direction, step, chunk],
                at(section, right if direction == 0 else left, x, y),
            )

        return one

    def step_hop(direction, step):
        owner = (z + NZ - step) % NZ if direction == 0 else (z + step) % NZ
        piece = w_step.at[:16, pl.ds(pl.multiple_of(owner * LEN, LEN), LEN)]
        return remote(
            piece,
            piece,
            step_send.at[direction, step],
            step_recv.at[direction, step],
            at(section, right if direction == 0 else left, x, y),
        )

    in_hop = hop(w_in, True, in_send, in_recv)
    out_hop = hop(w_out, False, wout_send, wout_recv)
    relay_hop = hop(relay, False, relay_send, relay_recv)

    def pieces(step):
        half = CHUNKS // 2
        return [
            (chunk, direction)
            for chunk in range(CHUNKS)
            for direction in range(2)
            if step < 3 or chunk // half == direction
        ]

    def ring_start(one):
        if one is in_hop:
            for direction in range(2):
                step_hop(direction, 0).start()
        for chunk, direction in pieces(0):
            one(direction, 0, chunk).start()

    def ring_step(one, step):
        if one is in_hop:
            for direction in range(2):
                step_hop(direction, step - 1).wait_recv()
                if step < 3 or direction == 0:
                    step_hop(direction, step).start()
        for chunk, direction in pieces(0):
            one(direction, step - 1, chunk).wait_recv()
            if (chunk, direction) in pieces(step):
                one(direction, step, chunk).start()

    def ring_middle(one, arrived=None):
        for step in range(1, 4):
            ring_step(one, step)
            if arrived is not None:
                arrived(step)

    def ring_end(one):
        if one is in_hop:
            step_hop(0, 3).wait_recv()
        for chunk, direction in pieces(3):
            one(direction, 3, chunk).wait_recv()

    def ring_drain(one):
        for step in range(4):
            if one is in_hop:
                for direction in range(2 if step < 3 else 1):
                    step_hop(direction, step).wait_send()
            for chunk, direction in pieces(step):
                one(direction, step, chunk).wait_send()

    def own_out():
        return remote(
            w_out.at[:, own_block], relay.at[:, own_block], own_send, own_recv, sibling
        )

    def push(step):
        columns = pl.ds(pl.multiple_of((z + step) % NZ * LEN, LEN), LEN)
        return remote(
            relay.at[:, columns],
            w_out.at[:, columns],
            push_send.at[step],
            push_recv.at[step],
            sibling,
        )

    def push_both(step):
        push(step).start()
        push(NZ - step).start()

    loads[0].wait()

    @pl.when(section == 0)
    def _():
        own_out().start()

    for load in loads[1:]:
        load.wait()
    w_step[16:, :] = jnp.zeros((LEN - 16, NZ * LEN), BF16)
    def first(m, dx, dy):
        to_x = (x + dx) % NX
        to_y = (y + dy) % NY
        return remote(
            staged.at[m, to_x],
            act.at[m, y, pl.ds(pl.multiple_of(x * LEN, LEN), LEN), :],
            first_send.at[m, dx, dy],
            first_recv.at[m, dx, dy],
            at(0, z, to_x, to_y),
        )

    @pl.when(section == 0)
    def _():
        ring_start(in_hop)
        for m in range(MICRO):
            for xx in range(NX):
                for half in range(2):
                    stage(m, xx, half).wait()
            act[m, y, pl.ds(pl.multiple_of(x * LEN, LEN), LEN), :] = staged[m, x]
            for dx in range(NX):
                for dy in range(NY):
                    if dx or dy:
                        first(m, dx, dy).start()
        ring_middle(in_hop)
        pl.semaphore_signal(go_sem, inc=1, device_id=sibling, device_id_type=MESH)

    @pl.when(section == 1)
    def _():
        own_out().wait_recv()
        pl.semaphore_wait(go_sem, 1)
        ring_start(relay_hop)
        ring_middle(relay_hop, push_both)
        ring_start(in_hop)
        ring_end(relay_hop)
        push(NZ // 2).start()
        ring_middle(in_hop)
        ring_start(out_hop)
        ring_end(in_hop)

    def block(ahead):
        return pl.ds(pl.multiple_of((x + ahead) % NX * LEN, LEN), LEN)

    def order(i):
        return i + i // 2 - i // 3 * 2

    def onward(m, ahead, dy):
        return remote(
            h_next.at[m, block(ahead), :],
            act.at[m, y, block(ahead), :],
            next_send.at[m, ahead, dy],
            next_recv.at[m, ahead, dy],
            at(1 - section, z, x, (y + dy) % NY),
        )

    def towards(direction):
        return at(section, z, (x + 1 + 2 * direction) % NX, y)

    def half_block(ahead, half):
        return pl.ds(pl.multiple_of((x + ahead) % NX * LEN + half * HALF, HALF), HALF)

    def send_hop(m, direction):
        return remote(
            part.at[m, half_block(2, direction), :],
            hop_got.at[m, direction],
            hop_send.at[m, direction],
            hop_recv.at[m, direction],
            towards(direction),
        )

    def send_part(m, direction, half):
        return remote(
            part.at[m, half_block(1 + 2 * direction, half), :],
            got.at[m, direction, pl.ds(half * HALF, HALF), :],
            part_send.at[m, direction, half],
            part_recv.at[m, direction, half],
            towards(direction),
        )

    def fold(m):
        for direction in range(2):
            send_hop(m, direction).wait_recv()
            rows = half_block(1 + 2 * direction, direction)
            for c in range(COLS // LEN):
                cols = slice(c * LEN, (c + 1) * LEN)
                part[m, rows, cols] = (
                    part[m, rows, cols].astype(F32) + hop_got[m, direction, :, cols].astype(F32)
                ).astype(BF16)
            send_part(m, direction, direction).start()

    def send_y(m, direction, half):
        piece = y_all.at[m, x, pl.ds(half * HALF, HALF), :]
        return remote(
            piece,
            piece,
            y_send.at[m, direction, half],
            y_recv.at[m, direction, half],
            towards(direction),
        )

    def pass_y(m, direction):
        piece = y_all.at[m, (x + 3 - 2 * direction) % NX, pl.ds(direction * HALF, HALF), :]
        return remote(
            piece,
            piece,
            pass_send.at[m, direction],
            pass_recv.at[m, direction],
            towards(direction),
        )

    def pass_on(m):
        for direction in range(2):
            send_y(m, direction, direction).wait_recv()
            pass_y(m, direction).start()

    def wait_y(m, ahead):
        @pl.when(ahead == 1)
        def _():
            send_y(m, 1, 0).wait_recv()

        @pl.when(ahead == 3)
        def _():
            send_y(m, 0, 1).wait_recv()

        @pl.when(ahead == 2)
        def _():
            for direction in range(2):
                pass_y(m, direction).wait_recv()

    def send_proj(m, ahead, dy):
        to_y = (y + dy) % NY
        return remote(
            proj.at[m, to_y, block(ahead), :],
            proj_got.at[m, dy, block(ahead), :],
            proj_send.at[m, ahead, dy],
            proj_recv.at[m, ahead, dy],
            at(section, z, x, to_y),
        )

    def send_out(m, ahead, half):
        return remote(
            h_next.at[m, block(ahead), pl.ds(half * LEN, LEN)],
            out_ref.at[0, m, 0, :, pl.ds(pl.multiple_of((x + NX * half) * LEN, LEN), LEN)],
            out_send.at[m, ahead, half],
            out_recv.at[m, ahead, half],
            at(section, z, (x + ahead) % NX, y),
        )

    lane = lax.broadcasted_iota(jnp.int32, (LEN, LEN), 1)
    row = lax.broadcasted_iota(jnp.int32, (LEN, LEN), 0)

    def prepare(m, ahead):
        def scale(i, carry):
            rows = pl.ds(pl.multiple_of((x + ahead) % NX * LEN + i * 64, 64), 64)
            total = jnp.zeros((64, LEN), F32)
            for yy in range(NY):
                for half in range(2):
                    at_ = yy * 2 * LEN + half * LEN
                    value = act[m, yy, rows, half * LEN : (half + 1) * LEN].astype(F32)
                    total = total + value * value
                    gain = gains[
                        :, pl.ds(pl.multiple_of((yy * 2 + half) * NX * LEN + x * LEN, LEN), LEN)
                    ]
                    scaled[m, rows, at_ : at_ + LEN] = (value * gain).astype(BF16)
            squares[m, rows, :] = jnp.broadcast_to(
                jnp.sum(total, axis=1, keepdims=True), (64, LEN)
            )
            return carry

        lax.fori_loop(0, LEN // 64, scale, 0)

    def project_in(m, ahead):
        rows = block(ahead)
        values = scaled[m, rows, :]
        for c in range((WIDTH + BC) // 256):
            cols = slice(c * 256, (c + 1) * 256)
            part[m, rows, cols] = jnp.dot(
                values, w_in[:, cols], preferred_element_type=F32
            ).astype(BF16)
        small = lax.dot_general(
            values, w_step[...], (((1,), (1,)), ((), ())), preferred_element_type=F32
        )
        high = small.astype(BF16).astype(F32)
        low = small - high
        square = squares[m, rows, :]
        square_high = square.astype(BF16).astype(F32)
        packed = high + pltpu.roll(low, 16, 1)
        packed = jnp.where(lane == 32, square_high, packed)
        packed = jnp.where(lane == 33, square - square_high, packed)
        part[m, rows, WIDTH + BC :] = packed.astype(BF16)

        @pl.when(ahead == 2)
        def _():
            for direction in range(2):
                send_hop(m, direction).start()

        for direction in range(2):

            @pl.when(ahead == 1 + 2 * direction)
            def _(direction=direction):
                send_part(m, direction, 1 - direction).start()

    def mix(m):
        for half in range(2):
            for direction in range(2):
                send_part(m, direction, half).wait_recv()
        own = block(0)

        def summed(cols):
            total = part[m, own, cols].astype(F32)
            for direction in range(2):
                total = total + got[m, direction, :, cols].astype(F32)
            return total

        tail = summed(slice(WIDTH + BC, COLS))
        square = tail[:, 32:33] + tail[:, 33:34]
        inverse = lax.rsqrt(square * (1.0 / (NX * WIDTH)) + EPS)
        raw = (tail + pltpu.roll(tail, LEN - 16, 1)) * inverse
        pre = raw + jnp.concatenate([biases[...], jnp.zeros((1, LEN - 16), F32)], axis=1)
        steps = jnp.maximum(pre, 0.0) + jnp.log1p(jnp.exp(-jnp.abs(pre)))
        steps = jnp.where(lane < 16, steps, 0.0)
        lower = jnp.where(row >= lane, 1.0, 0.0)
        decay = jnp.dot(
            lower,
            steps * jnp.concatenate([rates[...], jnp.zeros((1, LEN - 16), F32)], axis=1),
            precision=lax.Precision.HIGHEST,
            preferred_element_type=F32,
        )
        decay_t = decay.T
        inverse_wide = jnp.broadcast_to(inverse, (LEN, LEN))

        padded[0:8, :] = jnp.zeros((8, LEN), F32)

        for c in range((WIDTH + BC) // LEN):
            cols = slice(c * LEN, (c + 1) * LEN)
            padded[8:, :] = summed(cols) * inverse_wide
            value = jnp.zeros((LEN, LEN), F32)
            for tap in range(4):
                value = value + taps[tap : tap + 1, cols] * padded[5 + tap : 5 + tap + LEN, :]
            conv[:, cols] = value / (1.0 + jnp.exp(-value))

        scores = lax.dot_general(
            conv[:, WIDTH + STATE : WIDTH + BC],
            conv[:, WIDTH : WIDTH + STATE],
            (((1,), (1,)), ((), ())),
            precision=lax.Precision.HIGHEST,
            preferred_element_type=F32,
        )
        scores = jnp.where(row >= lane, scores, 0.0)
        power = jnp.zeros((LEN, LEN), F32)
        for pair in range(WIDTH // LEN):
            cols = slice(pair * LEN, (pair + 1) * LEN)
            mixes = []
            for j in (2 * pair, 2 * pair + 1):
                gap = jnp.minimum(decay_t[j : j + 1, :] - decay[:, j : j + 1], 0.0)
                mixes.append((jnp.exp(gap) * scores).astype(BF16))
            value = conv[:, cols]
            step = jnp.where(
                lane < HEAD_DIM,
                steps[:, 2 * pair : 2 * pair + 1],
                steps[:, 2 * pair + 1 : 2 * pair + 2],
            )
            stepped = value * step
            blocks = jnp.concatenate(
                [
                    jnp.where(lane < HEAD_DIM, stepped, 0.0).astype(BF16),
                    jnp.where(lane < HEAD_DIM, 0.0, stepped).astype(BF16),
                ],
                axis=0,
            )
            mixed = jnp.dot(
                jnp.concatenate(mixes, axis=1), blocks, preferred_element_type=F32
            )
            skip = jnp.where(
                lane[:1] < HEAD_DIM,
                skips[:, 2 * pair : 2 * pair + 1],
                skips[:, 2 * pair + 1 : 2 * pair + 2],
            )
            mixed = mixed + skip * value
            power = power + mixed * mixed
            y_raw[:, cols] = mixed
        norm = lax.rsqrt(jnp.sum(power, axis=1, keepdims=True) * (1.0 / WIDTH) + EPS)
        norm = jnp.broadcast_to(norm, (LEN, LEN))
        for c in range(WIDTH // LEN):
            cols = slice(c * LEN, (c + 1) * LEN)
            y_all[m, x, :, cols] = (y_raw[:, cols] * norm * y_gains[:, cols]).astype(BF16)
        for half in range(2):
            for direction in range(2):
                send_y(m, direction, (direction + half) % 2).start()

    def project_out(m, ahead):
        values = y_all[m, (x + ahead) % NX]
        for dy in (1, 3, 2, 0):
            to_y = (y + dy) % NY
            cols = pl.ds(pl.multiple_of(to_y * 2 * LEN, 2 * LEN), 2 * LEN)
            proj[m, to_y, block(ahead), :] = jnp.dot(
                values, w_out[:, cols], preferred_element_type=F32
            ).astype(BF16)
            if dy:
                send_proj(m, ahead, dy).start()

    def give(m, ahead):
        rows = block(ahead)

        @pl.when(ahead != 0)
        def _():
            for half in range(2):
                send_out(m, ahead, half).start()

        @pl.when(ahead == 0)
        def _():
            for half in range(2):
                out_ref[
                    0, m, 0, :, pl.ds(pl.multiple_of((x + NX * half) * LEN, LEN), LEN)
                ] = h_next[m, rows, half * LEN : (half + 1) * LEN]

    def finish(m, ahead):
        for dy in (1, 3, 2):
            send_proj(m, ahead, dy).wait_recv()
        rows = block(ahead)
        total = proj[m, y, rows, :].astype(F32)
        for dy in (1, 2, 3):
            total = total + proj_got[m, dy, rows, :].astype(F32)
        h_next[m, rows, :] = (act[m, y, rows, :].astype(F32) + total).astype(BF16)

        @pl.when(section == 0)
        def _():
            for dy in (1, 3, 2, 0):
                onward(m, ahead, dy).start()

        pl.when(section == 1)(lambda: give(m, ahead))

    @pl.when(section == 0)
    def _():
        for m in range(MICRO):
            for dx in range(NX):
                for dy in range(NY):
                    if dx or dy:
                        first(m, dx, dy).wait_recv()

        def all_rows(i, carry):
            prepare(i // NX, i % NX)
            return carry

        lax.fori_loop(0, MICRO * NX, all_rows, 0)
        ring_end(in_hop)

    def rows_in(i, carry):
        m = i // NX
        turn = i % NX
        ahead = order(jnp.where(section == 0, NX - 1 - turn, turn))

        @pl.when(section == 1)
        def _():
            for dy in range(NY):
                onward(m, ahead, dy).wait_recv()
            prepare(m, ahead)

        project_in(m, ahead)
        return carry

    def second(work):
        pl.when(section == 1)(work)

    lax.fori_loop(0, NX, rows_in, 0)
    second(lambda: ring_step(out_hop, 1))
    lax.fori_loop(NX, NX + 1, rows_in, 0)
    fold(0)
    second(lambda: ring_step(out_hop, 2))
    lax.fori_loop(NX + 1, MICRO * NX, rows_in, 0)
    second(lambda: ring_step(out_hop, 3))
    pl.when(section == 0)(lambda: fold(1))

    def stage_mix(m, carry):
        mix(m)

        @pl.when(m == 0)
        def _():
            @pl.when(section == 0)
            def _():
                for step in range(1, NZ):
                    push(step).wait_recv()

            @pl.when(section == 1)
            def _():
                fold(1)
                ring_end(out_hop)

        project_out(m, 0)
        pl.when(jnp.where(section == 0, m == 1, m == 0))(lambda: pass_on(0))
        return carry

    lax.fori_loop(0, MICRO, stage_mix, 0)
    finish(0, 0)

    def stage_end(i, carry):
        behind = jnp.maximum(i - 1, 0)
        finish(
            jnp.where(i == 0, 1, behind // (NX - 1)),
            jnp.where(i == 0, 0, order(behind % (NX - 1) + 1)),
        )
        return carry

    def ended(i):
        return jnp.where(i < 2, 0, jnp.where(i < 4, 3, jnp.where(i < 5, 4, 7)))

    def stage_out(i, carry):
        m = i // (NX - 1)
        ahead = order(i % (NX - 1) + 1)
        wait_y(m, ahead)
        project_out(m, ahead)
        pl.when(i == NX - 2)(lambda: pass_on(1))
        lax.fori_loop(ended(i - 1), ended(i), stage_end, 0)
        return carry

    lax.fori_loop(0, MICRO * (NX - 1), stage_out, 0)

    @pl.when(section == 0)
    def _():
        def later(i, carry):
            give(i // NX, i % NX)
            return carry

        lax.fori_loop(0, MICRO * NX, later, 0)

    def drain(m, carry):
        for ahead in (1, 2, 3):
            for half in range(2):
                send_out(m, ahead, half).wait()
        for direction in range(2):
            for half in range(2):
                send_part(m, direction, half).wait_send()
                send_y(m, direction, half).wait_send()
            send_hop(m, direction).wait_send()
            pass_y(m, direction).wait_send()
        for ahead in range(NX):
            for dy in (1, 2, 3):
                send_proj(m, ahead, dy).wait_send()

        @pl.when(section == 0)
        def _():
            for ahead in range(NX):
                for dy in range(NY):
                    onward(m, ahead, dy).wait_send()
                    if ahead or dy:
                        first(m, ahead, dy).wait_send()

        return carry

    lax.fori_loop(0, MICRO, drain, 0)
    ring_drain(in_hop)

    @pl.when(section == 0)
    def _():
        own_out().wait_send()

    @pl.when(section == 1)
    def _():
        ring_drain(relay_hop)
        ring_drain(out_hop)
        for step in range(1, NZ):
            push(step).wait_send()


def body(
    stream, norm_gain, w_x, w_bc, w_dt, conv_x, conv_bc, dt_bias, decay_rate, skip_d, y_gain, w_out
):
    vmem = pl.BlockSpec(memory_space=pltpu.VMEM)
    whole = pl.BlockSpec(memory_space=pltpu.HBM)
    dma = pltpu.SemaphoreType.DMA
    return pl.pallas_call(
        kernel,
        out_shape=jax.ShapeDtypeStruct((1, MICRO, 1, LEN, WIDTH), BF16),
        in_specs=[whole] * 12,
        out_specs=vmem,
        scratch_shapes=[
            pltpu.VMEM((MICRO, NX, LEN, 2 * LEN), BF16),
            pltpu.VMEM((1, NX * WIDTH), F32),
            pltpu.VMEM((4, WIDTH + BC), F32),
            pltpu.VMEM((1, 16), F32),
            pltpu.VMEM((1, 16), F32),
            pltpu.VMEM((1, 16), F32),
            pltpu.VMEM((1, WIDTH), F32),
            pltpu.VMEM((NZ * LEN, WIDTH + BC), BF16),
            pltpu.VMEM((WIDTH, NZ * LEN), BF16),
            pltpu.VMEM((WIDTH, NZ * LEN), BF16),
            pltpu.VMEM((LEN, NZ * LEN), BF16),
            pltpu.VMEM((MICRO, NY, ROWS, 2 * LEN), BF16),
            pltpu.VMEM((MICRO, ROWS, WIDTH), BF16),
            pltpu.VMEM((MICRO, ROWS, COLS), BF16),
            pltpu.VMEM((MICRO, 2, LEN, COLS), BF16),
            pltpu.VMEM((MICRO, 2, HALF, COLS), BF16),
            pltpu.VMEM((8 + LEN, LEN), F32),
            pltpu.VMEM((LEN, WIDTH + BC), F32),
            pltpu.VMEM((LEN, WIDTH), F32),
            pltpu.VMEM((MICRO, NX, LEN, WIDTH), BF16),
            pltpu.VMEM((MICRO, NY, ROWS, 2 * LEN), BF16),
            pltpu.VMEM((MICRO, NY, ROWS, 2 * LEN), BF16),
            pltpu.VMEM((MICRO, ROWS, 2 * LEN), BF16),
            pltpu.VMEM((MICRO, ROWS, LEN), F32),
            dma((2, 4, CHUNKS)),
            dma((2, 4, CHUNKS)),
            dma((2, 4)),
            dma((2, 4)),
            dma((2, 4, CHUNKS)),
            dma((2, 4, CHUNKS)),
            dma((MICRO, NX, NY)),
            dma((MICRO, NX, NY)),
            dma((MICRO, NX, NY)),
            dma((MICRO, NX, NY)),
            dma((MICRO, 2)),
            dma((MICRO, 2)),
            dma((MICRO, 2, 2)),
            dma((MICRO, 2, 2)),
            dma((MICRO, 2, 2)),
            dma((MICRO, 2, 2)),
            dma((MICRO, 2)),
            dma((MICRO, 2)),
            dma((MICRO, NX, NY)),
            dma((MICRO, NX, NY)),
            dma((MICRO, NX, 2)),
            dma((MICRO, NX, 2)),
            dma((2, 4, CHUNKS)),
            dma((2, 4, CHUNKS)),
            dma((NZ,)),
            dma((NZ,)),
            dma,
            dma,
            dma((11,)),
            dma((MICRO, NX, 2)),
            pltpu.SemaphoreType.REGULAR,
        ],
        compiler_params=pltpu.CompilerParams(
            collective_id=0, has_side_effects=True, vmem_limit_bytes=60 * 1024 * 1024
        ),
        name="mixer",
    )(
        stream,
        norm_gain,
        w_x,
        w_bc,
        jnp.swapaxes(w_dt, 1, 2),
        conv_x,
        conv_bc,
        dt_bias,
        decay_rate,
        skip_d,
        y_gain,
        w_out,
    )


def solution(mesh):
    in_specs = (
        P(None, "dp", None, "head"),
        P("section", None),
        P("section", "dp", "head"),
        P("section", "dp", "head"),
        P("section", "dp", "head"),
        P("section", None, "head"),
        P("section", None, "head"),
        P("section", "head"),
        P("section", "head"),
        P("section", "head"),
        P("section", "head"),
        P("section", "head", "dp"),
    )
    out_specs = P("section", None, "dp", None, "head")
    return jax.shard_map(body, mesh=mesh, in_specs=in_specs, out_specs=out_specs, check_vma=False)
```

```python
import functools

import jax
import jax.numpy as jnp
from jax import lax
from jax.experimental import pallas as pl
from jax.experimental.pallas import tpu as pltpu
from jax.sharding import PartitionSpec as P

MESH = pl.DeviceIdType.MESH
HEAD_DIM = 64
STATE = 128
NX = 4
NY = 4
NZ = 8
MICRO = 2
LEN = 128
ROWS = NX * LEN
WIDTH = 1024
BC = 2 * STATE
COLS = WIDTH + BC + 128
CHUNKS = 4
HALF = LEN // 2
EPS = 1e-05
F32 = jnp.float32
BF16 = jnp.bfloat16


def remote(src, dst, send_sem, recv_sem, device):
    return pltpu.make_async_remote_copy(
        src_ref=src,
        dst_ref=dst,
        send_sem=send_sem,
        recv_sem=recv_sem,
        device_id=device,
        device_id_type=MESH,
    )


def kernel(
    stream_ref,
    gain_ref,
    w_x_ref,
    w_bc_ref,
    w_dt_ref,
    conv_x_ref,
    conv_bc_ref,
    bias_ref,
    rate_ref,
    skip_ref,
    y_gain_ref,
    w_out_ref,
    out_ref,
    staged,
    gains,
    taps,
    biases,
    rates,
    skips,
    y_gains,
    w_in,
    w_out,
    relay,
    w_step,
    act,
    scaled,
    part,
    got,
    hop_got,
    far_got,
    padded,
    conv,
    y_raw,
    y_all,
    proj,
    proj_got,
    h_next,
    squares,
    in_send,
    in_recv,
    step_send,
    step_recv,
    wout_send,
    wout_recv,
    first_send,
    first_recv,
    next_send,
    next_recv,
    hop_send,
    hop_recv,
    far_send,
    far_recv,
    part_send,
    part_recv,
    y_send,
    y_recv,
    pass_send,
    pass_recv,
    proj_send,
    proj_recv,
    out_send,
    out_recv,
    relay_send,
    relay_recv,
    push_send,
    push_recv,
    own_send,
    own_recv,
    load_sem,
    stream_sem,
    keep_sem,
    go_sem,
):
    section = lax.axis_index("section")
    dp = lax.axis_index("dp")
    y = lax.axis_index("head")
    z = dp // NX
    x = dp % NX

    def at(s, zz, xx, yy):
        return (s, zz * NX + xx, yy)

    right, left = (z + 1) % NZ, (z + NZ - 1) % NZ
    sibling = at(1 - section, z, x, y)
    own_block = pl.ds(pl.multiple_of(z * LEN, LEN), LEN)

    loads = [
        pltpu.make_async_copy(source, target, load_sem.at[i])
        for i, (source, target) in enumerate(
            [
                (w_out_ref.at[0], w_out.at[:, own_block]),
                (w_x_ref.at[0], w_in.at[own_block, :WIDTH]),
                (w_bc_ref.at[0], w_in.at[own_block, WIDTH : WIDTH + BC]),
                (w_dt_ref.at[0], w_step.at[:16, own_block]),
                (gain_ref, gains),
                (conv_x_ref.at[0], taps.at[:, :WIDTH]),
                (conv_bc_ref.at[0], taps.at[:, WIDTH:]),
                (bias_ref, biases),
                (rate_ref, rates),
                (skip_ref, skips),
                (y_gain_ref, y_gains),
            ]
        )
    ]
    for load in loads:
        load.start()

    def stage(m, xx, half):
        return pltpu.make_async_copy(
            stream_ref.at[m, 0, :, pl.ds(pl.multiple_of((xx + NX * half) * LEN, LEN), LEN)],
            staged.at[m, xx, :, pl.ds(half * LEN, LEN)],
            stream_sem.at[m, xx, half],
        )

    @pl.when(section == 0)
    def _():
        def work(i, carry):
            for half in range(2):
                stage(i // NX, i % NX, half).start()
            return carry

        lax.fori_loop(0, MICRO * NX, work, 0)

    barrier = pltpu.get_barrier_semaphore()
    for dx in range(NX):
        for dy in range(NY):
            if dx or dy:
                pl.semaphore_signal(
                    barrier,
                    inc=1,
                    device_id=at(section, z, (x + dx) % NX, (y + dy) % NY),
                    device_id_type=MESH,
                )
    for dy in range(NY):
        pl.semaphore_signal(
            barrier, inc=1, device_id=at(1 - section, z, x, (y + dy) % NY), device_id_type=MESH
        )
    for zz in (right, left):
        pl.semaphore_signal(
            barrier, inc=1, device_id=at(section, zz, x, y), device_id_type=MESH
        )
    pl.semaphore_wait(barrier, NX * NY - 1 + NY + 2)

    def hop(buffer, by_rows, sends, receives):
        def one(direction, step, chunk):
            owner = (z + NZ - step) % NZ if direction == 0 else (z + step) % NZ
            if by_rows:
                size = LEN // CHUNKS
                piece = buffer.at[pl.ds(pl.multiple_of(owner * LEN + chunk * size, size), size)]
            else:
                size = WIDTH // CHUNKS
                piece = buffer.at[
                    pl.ds(chunk * size, size), pl.ds(pl.multiple_of(owner * LEN, LEN), LEN)
                ]
            return remote(
                piece,
                piece,
                sends.at[direction, step, chunk],
                receives.at[direction, step, chunk],
                at(section, right if direction == 0 else left, x, y),
            )

        return one

    def step_hop(direction, step):
        owner = (z + NZ - step) % NZ if direction == 0 else (z + step) % NZ
        piece = w_step.at[:16, pl.ds(pl.multiple_of(owner * LEN, LEN), LEN)]
        return remote(
            piece,
            piece,
            step_send.at[direction, step],
            step_recv.at[direction, step],
            at(section, right if direction == 0 else left, x, y),
        )

    in_hop = hop(w_in, True, in_send, in_recv)
    out_hop = hop(w_out, False, wout_send, wout_recv)
    relay_hop = hop(relay, False, relay_send, relay_recv)

    def loop(count, work):
        def one(i, carry):
            work(i)
            return carry

        lax.fori_loop(0, count, one, 0)

    def ring_start(one):
        if one is in_hop:
            for direction in range(2):
                step_hop(direction, 0).start()

        def work(chunk):
            for direction in range(2):
                one(direction, 0, chunk).start()

        loop(CHUNKS, work)

    def ring_step(one, step):
        if one is in_hop:
            for direction in range(2):
                step_hop(direction, step - 1).wait_recv()
                step_hop(direction, step).start()

        def work(chunk):
            for direction in range(2):
                one(direction, step - 1, chunk).wait_recv()
                one(direction, step, chunk).start()

        loop(CHUNKS, work)

    def ring_last(one):
        if one is in_hop:
            for direction in range(2):
                step_hop(direction, 2).wait_recv()
            step_hop(0, 3).start()

        def work(chunk):
            for direction in range(2):
                one(direction, 2, chunk).wait_recv()
                pl.when(chunk // (CHUNKS // 2) == direction)(
                    lambda direction=direction: one(direction, 3, chunk).start()
                )

        loop(CHUNKS, work)

    def ring_middle(one, arrived=None):
        def work(i):
            ring_step(one, i + 1)
            if arrived is not None:
                arrived(i + 1)

        loop(2, work)
        ring_last(one)
        if arrived is not None:
            arrived(3)

    def ring_end(one):
        if one is in_hop:
            step_hop(0, 3).wait_recv()
        for direction in range(2):
            loop(
                CHUNKS // 2,
                lambda i, direction=direction: one(
                    direction, 3, direction * (CHUNKS // 2) + i
                ).wait_recv(),
            )

    def ring_drain(one):
        if one is in_hop:
            for step in range(4):
                for direction in range(2 if step < 3 else 1):
                    step_hop(direction, step).wait_send()

        def work(i):
            for direction in range(2):
                one(direction, i // CHUNKS, i % CHUNKS).wait_send()

        loop(3 * CHUNKS, work)
        for direction in range(2):
            loop(
                CHUNKS // 2,
                lambda i, direction=direction: one(
                    direction, 3, direction * (CHUNKS // 2) + i
                ).wait_send(),
            )

    def own_out():
        return remote(
            w_out.at[:, own_block], relay.at[:, own_block], own_send, own_recv, sibling
        )

    def push(step):
        columns = pl.ds(pl.multiple_of((z + step) % NZ * LEN, LEN), LEN)
        return remote(
            relay.at[:, columns],
            w_out.at[:, columns],
            push_send.at[step],
            push_recv.at[step],
            sibling,
        )

    def push_both(step):
        push(step).start()
        push(NZ - step).start()

    loads[0].wait()

    @pl.when(section == 0)
    def _():
        own_out().start()

    for load in loads[1:]:
        load.wait()
    w_step[16:, :] = jnp.zeros((LEN - 16, NZ * LEN), BF16)
    def first(m, dx, dy):
        to_x = (x + dx) % NX
        to_y = (y + dy) % NY
        return remote(
            staged.at[m, to_x],
            act.at[m, y, pl.ds(pl.multiple_of(x * LEN, LEN), LEN), :],
            first_send.at[m, dx, dy],
            first_recv.at[m, dx, dy],
            at(0, z, to_x, to_y),
        )

    def block(ahead):
        return pl.ds(pl.multiple_of((x + ahead) % NX * LEN, LEN), LEN)

    def order(i):
        return i + i // 2 - i // 3 * 2

    def onward(m, ahead, dy):
        return remote(
            h_next.at[m, block(ahead), :],
            act.at[m, y, block(ahead), :],
            next_send.at[m, ahead, dy],
            next_recv.at[m, ahead, dy],
            at(1 - section, z, x, (y + dy) % NY),
        )

    def towards(direction):
        return at(section, z, (x + 1 + 2 * direction) % NX, y)

    def half_block(ahead, half):
        return pl.ds(pl.multiple_of((x + ahead) % NX * LEN + half * HALF, HALF), HALF)

    def send_hop(m, direction):
        return remote(
            part.at[m, half_block(2, direction), :],
            hop_got.at[m, direction],
            hop_send.at[m, direction],
            hop_recv.at[m, direction],
            towards(direction),
        )

    def send_far(m):
        return remote(
            part.at[m, block(2), :],
            far_got.at[m],
            far_send.at[m],
            far_recv.at[m],
            at(section, z, (x + 2) % NX, y),
        )

    def send_part(m, direction, half):
        return remote(
            part.at[m, half_block(1 + 2 * direction, half), :],
            got.at[m, direction, pl.ds(half * HALF, HALF), :],
            part_send.at[m, direction, half],
            part_recv.at[m, direction, half],
            towards(direction),
        )

    def fold(m):
        for direction in range(2):
            send_hop(m, direction).wait_recv()
            rows = half_block(1 + 2 * direction, direction)
            for c in range(COLS // LEN):
                cols = slice(c * LEN, (c + 1) * LEN)
                part[m, rows, cols] = (
                    part[m, rows, cols].astype(F32) + hop_got[m, direction, :, cols].astype(F32)
                ).astype(BF16)
            send_part(m, direction, direction).start()

    def send_y(m, direction, half):
        piece = y_all.at[m, x, pl.ds(half * HALF, HALF), :]
        return remote(
            piece,
            piece,
            y_send.at[m, direction, half],
            y_recv.at[m, direction, half],
            towards(direction),
        )

    def pass_y(m, direction):
        piece = y_all.at[m, (x + 3 - 2 * direction) % NX, pl.ds(direction * HALF, HALF), :]
        return remote(
            piece,
            piece,
            pass_send.at[m, direction],
            pass_recv.at[m, direction],
            towards(direction),
        )

    def pass_on(m):
        for direction in range(2):
            send_y(m, direction, direction).wait_recv()
            pass_y(m, direction).start()

    def wait_y(m, ahead):
        @pl.when(ahead == 1)
        def _():
            send_y(m, 1, 0).wait_recv()

        @pl.when(ahead == 3)
        def _():
            send_y(m, 0, 1).wait_recv()

        @pl.when(ahead == 2)
        def _():
            for direction in range(2):
                pass_y(m, direction).wait_recv()

    def send_proj(m, ahead, dy):
        to_y = (y + dy) % NY
        return remote(
            proj.at[m, to_y, block(ahead), :],
            proj_got.at[m, dy, block(ahead), :],
            proj_send.at[m, ahead, dy],
            proj_recv.at[m, ahead, dy],
            at(section, z, x, to_y),
        )

    def send_out(m, ahead, half):
        return remote(
            h_next.at[m, block(ahead), pl.ds(half * LEN, LEN)],
            out_ref.at[0, m, 0, :, pl.ds(pl.multiple_of((x + NX * half) * LEN, LEN), LEN)],
            out_send.at[m, ahead, half],
            out_recv.at[m, ahead, half],
            at(section, z, (x + ahead) % NX, y),
        )

    lane = lax.broadcasted_iota(jnp.int32, (LEN, LEN), 1)
    row = lax.broadcasted_iota(jnp.int32, (LEN, LEN), 0)

    def prepare(m, ahead):
        def scale(i, carry):
            rows = pl.ds(pl.multiple_of((x + ahead) % NX * LEN + i * 64, 64), 64)
            total = jnp.zeros((64, LEN), F32)
            for yy in range(NY):
                for half in range(2):
                    at_ = yy * 2 * LEN + half * LEN
                    value = act[m, yy, rows, half * LEN : (half + 1) * LEN].astype(F32)
                    total = total + value * value
                    gain = gains[
                        :, pl.ds(pl.multiple_of((yy * 2 + half) * NX * LEN + x * LEN, LEN), LEN)
                    ]
                    scaled[m, rows, at_ : at_ + LEN] = (value * gain).astype(BF16)
            squares[m, rows, :] = jnp.broadcast_to(
                jnp.sum(total, axis=1, keepdims=True), (64, LEN)
            )
            return carry

        lax.fori_loop(0, LEN // 64, scale, 0)

    def project_in(m, ahead):
        rows = block(ahead)
        values = scaled[m, rows, :]
        for c in range((WIDTH + BC) // 256):
            cols = slice(c * 256, (c + 1) * 256)
            part[m, rows, cols] = jnp.dot(
                values, w_in[:, cols], preferred_element_type=F32
            ).astype(BF16)
        small = lax.dot_general(
            values, w_step[...], (((1,), (1,)), ((), ())), preferred_element_type=F32
        )
        high = small.astype(BF16).astype(F32)
        low = small - high
        square = squares[m, rows, :]
        square_high = square.astype(BF16).astype(F32)
        packed = high + pltpu.roll(low, 16, 1)
        packed = jnp.where(lane == 32, square_high, packed)
        packed = jnp.where(lane == 33, square - square_high, packed)
        part[m, rows, WIDTH + BC :] = packed.astype(BF16)

        @pl.when(ahead == 2)
        def _():
            @pl.when(section == 0)
            def _():
                for direction in range(2):
                    send_hop(m, direction).start()

            pl.when(section == 1)(lambda: send_far(m).start())

        for direction in range(2):

            @pl.when(ahead == 1 + 2 * direction)
            def _(direction=direction):
                send_part(m, direction, 1 - direction).start()
                pl.when(section == 1)(lambda: send_part(m, direction, direction).start())

    def mix(m):
        for half in range(2):
            for direction in range(2):
                send_part(m, direction, half).wait_recv()
        pl.when(section == 1)(lambda: send_far(m).wait_recv())
        own = block(0)

        def summed(cols):
            total = part[m, own, cols].astype(F32) + far_got[m, :, cols].astype(F32)
            for direction in range(2):
                total = total + got[m, direction, :, cols].astype(F32)
            return total

        tail = summed(slice(WIDTH + BC, COLS))
        square = tail[:, 32:33] + tail[:, 33:34]
        inverse = lax.rsqrt(square * (1.0 / (NX * WIDTH)) + EPS)
        raw = (tail + pltpu.roll(tail, LEN - 16, 1)) * inverse
        pre = raw + jnp.concatenate([biases[...], jnp.zeros((1, LEN - 16), F32)], axis=1)
        steps = jnp.maximum(pre, 0.0) + jnp.log1p(jnp.exp(-jnp.abs(pre)))
        steps = jnp.where(lane < 16, steps, 0.0)
        lower = jnp.where(row >= lane, 1.0, 0.0)
        decay = jnp.dot(
            lower,
            steps * jnp.concatenate([rates[...], jnp.zeros((1, LEN - 16), F32)], axis=1),
            precision=lax.Precision.HIGHEST,
            preferred_element_type=F32,
        )
        decay_t = decay.T
        inverse_wide = jnp.broadcast_to(inverse, (LEN, LEN))

        padded[0:8, :] = jnp.zeros((8, LEN), F32)

        for c in range((WIDTH + BC) // LEN):
            cols = slice(c * LEN, (c + 1) * LEN)
            padded[8:, :] = summed(cols) * inverse_wide
            value = jnp.zeros((LEN, LEN), F32)
            for tap in range(4):
                value = value + taps[tap : tap + 1, cols] * padded[5 + tap : 5 + tap + LEN, :]
            conv[:, cols] = value / (1.0 + jnp.exp(-value))

        scores = lax.dot_general(
            conv[:, WIDTH + STATE : WIDTH + BC],
            conv[:, WIDTH : WIDTH + STATE],
            (((1,), (1,)), ((), ())),
            precision=lax.Precision.HIGHEST,
            preferred_element_type=F32,
        )
        scores = jnp.where(row >= lane, scores, 0.0)
        power = jnp.zeros((LEN, LEN), F32)
        for pair in range(WIDTH // LEN):
            cols = slice(pair * LEN, (pair + 1) * LEN)
            mixes = []
            for j in (2 * pair, 2 * pair + 1):
                gap = jnp.minimum(decay_t[j : j + 1, :] - decay[:, j : j + 1], 0.0)
                mixes.append((jnp.exp(gap) * scores).astype(BF16))
            value = conv[:, cols]
            step = jnp.where(
                lane < HEAD_DIM,
                steps[:, 2 * pair : 2 * pair + 1],
                steps[:, 2 * pair + 1 : 2 * pair + 2],
            )
            stepped = value * step
            blocks = jnp.concatenate(
                [
                    jnp.where(lane < HEAD_DIM, stepped, 0.0).astype(BF16),
                    jnp.where(lane < HEAD_DIM, 0.0, stepped).astype(BF16),
                ],
                axis=0,
            )
            mixed = jnp.dot(
                jnp.concatenate(mixes, axis=1), blocks, preferred_element_type=F32
            )
            skip = jnp.where(
                lane[:1] < HEAD_DIM,
                skips[:, 2 * pair : 2 * pair + 1],
                skips[:, 2 * pair + 1 : 2 * pair + 2],
            )
            mixed = mixed + skip * value
            power = power + mixed * mixed
            y_raw[:, cols] = mixed
        norm = lax.rsqrt(jnp.sum(power, axis=1, keepdims=True) * (1.0 / WIDTH) + EPS)
        norm = jnp.broadcast_to(norm, (LEN, LEN))
        for c in range(WIDTH // LEN):
            cols = slice(c * LEN, (c + 1) * LEN)
            y_all[m, x, :, cols] = (y_raw[:, cols] * norm * y_gains[:, cols]).astype(BF16)
        for half in range(2):
            for direction in range(2):
                send_y(m, direction, (direction + half) % 2).start()

    def project_out(m, ahead):
        values = y_all[m, (x + ahead) % NX]
        for dy in (1, 3, 2, 0):
            to_y = (y + dy) % NY
            cols = pl.ds(pl.multiple_of(to_y * 2 * LEN, 2 * LEN), 2 * LEN)
            proj[m, to_y, block(ahead), :] = jnp.dot(
                values, w_out[:, cols], preferred_element_type=F32
            ).astype(BF16)
            if dy:
                send_proj(m, ahead, dy).start()

    def keep(m, half):
        return pltpu.make_async_copy(
            h_next.at[m, block(0), pl.ds(half * LEN, LEN)],
            out_ref.at[0, m, 0, :, pl.ds(pl.multiple_of((x + NX * half) * LEN, LEN), LEN)],
            keep_sem.at[m, half],
        )

    def give(m, ahead):
        rows = block(ahead)

        @pl.when(ahead != 0)
        def _():
            for half in range(2):
                send_out(m, ahead, half).start()

        @pl.when(ahead == 0)
        def _():
            for half in range(2):
                keep(m, half).start()

    def finish(m, ahead):
        for dy in (1, 3, 2):
            send_proj(m, ahead, dy).wait_recv()
        rows = block(ahead)
        total = proj[m, y, rows, :].astype(F32)
        for dy in (1, 2, 3):
            total = total + proj_got[m, dy, rows, :].astype(F32)
        h_next[m, rows, :] = (act[m, y, rows, :].astype(F32) + total).astype(BF16)

        @pl.when(section == 0)
        def _():
            for dy in (1, 3, 2, 0):
                onward(m, ahead, dy).start()

        pl.when(section == 1)(lambda: give(m, ahead))

    def plane(work):
        def one(i, carry):
            pl.when(i % (NX * NY) != 0)(
                lambda: work(i // (NX * NY), i // NY % NX, i % NY)
            )
            return carry

        lax.fori_loop(0, MICRO * NX * NY, one, 0)

    @pl.when(section == 1)
    def _():
        own_out().wait_recv()
        pl.semaphore_wait(go_sem, 1)
        ring_start(relay_hop)
        ring_middle(relay_hop, push_both)

    ring_start(in_hop)

    @pl.when(section == 0)
    def _():
        def arrange(m):
            def work(xx):
                for half in range(2):
                    stage(m, xx, half).wait()

            loop(NX, work)
            act[m, y, pl.ds(pl.multiple_of(x * LEN, LEN), LEN), :] = staged[m, x]

        loop(MICRO, arrange)
        plane(lambda m, dx, dy: first(m, dx, dy).start())
        for m in range(MICRO):
            far_got[m] = jnp.zeros((LEN, COLS), BF16)

    @pl.when(section == 1)
    def _():
        ring_end(relay_hop)
        push(NZ // 2).start()

    ring_middle(in_hop)

    @pl.when(section == 0)
    def _():
        pl.semaphore_signal(go_sem, inc=1, device_id=sibling, device_id_type=MESH)
        plane(lambda m, dx, dy: first(m, dx, dy).wait_recv())
        loop(MICRO * NX, lambda i: prepare(i // NX, i % NX))

    @pl.when(section == 1)
    def _():
        ring_start(out_hop)
        ring_drain(relay_hop)
        loop(NZ - 1, lambda step: push(step + 1).wait_send())

    ring_end(in_hop)
    pl.when(section == 1)(lambda: ring_drain(in_hop))

    def rows_in(i, carry):
        m = i // NX
        turn = i % NX
        ahead = order(jnp.where(section == 0, NX - 1 - turn, turn))

        @pl.when(section == 1)
        def _():
            for dy in range(NY):
                onward(m, ahead, dy).wait_recv()
            prepare(m, ahead)

        project_in(m, ahead)
        return carry

    def rows_and_more(i):
        rows_in(i, 0)
        pl.when(jnp.logical_and(section == 0, jnp.logical_or(i == NX, i == MICRO * NX - 1)))(
            lambda: fold(jnp.where(i == NX, 0, 1))
        )

        @pl.when(section == 1)
        def _():
            pl.when(jnp.logical_or(i == NX - 1, i == NX))(lambda: ring_step(out_hop, i - 2))
            pl.when(i == MICRO * NX - 1)(lambda: ring_last(out_hop))

    loop(MICRO * NX, rows_and_more)

    def unit(i):
        behind = jnp.maximum(i - 2, 0)
        return (
            jnp.where(i < 2, i, behind // (NX - 1)),
            jnp.where(i < 2, 0, order(behind % (NX - 1) + 1)),
        )

    def ended(i):
        return jnp.where(
            i < 1, 0, jnp.where(i < 4, 1, jnp.where(i < 6, 4, jnp.where(i < 7, 5, 8)))
        )

    def stage_out(i):
        m, ahead = unit(i)

        @pl.when(i < 2)
        def _():
            mix(m)

            @pl.when(m == 0)
            def _():
                @pl.when(section == 0)
                def _():
                    loop(NZ - 1, lambda step: push(step + 1).wait_recv())

                @pl.when(section == 1)
                def _():
                    ring_end(out_hop)

        @pl.when(i >= 2)
        def _():
            wait_y(m, ahead)

        project_out(m, ahead)
        pl.when(
            jnp.logical_or(i == jnp.where(section == 0, 1, 0), i == 4)
        )(lambda: pass_on(jnp.where(i == 4, 1, 0)))

        def end(k, carry):
            finish(*unit(k))
            return carry

        lax.fori_loop(ended(i - 1), ended(i), end, 0)

    loop(MICRO * NX, stage_out)

    @pl.when(section == 0)
    def _():
        def later(i, carry):
            give(i // NX, i % NX)
            return carry

        lax.fori_loop(0, MICRO * NX, later, 0)

    def drain(m):
        def outs(k):
            for half in range(2):
                send_out(m, k + 1, half).wait()

        loop(NX - 1, outs)

        def ways(direction):
            for half in range(2):
                send_part(m, direction, half).wait_send()
                send_y(m, direction, half).wait_send()
            pl.when(section == 0)(lambda: send_hop(m, direction).wait_send())
            pass_y(m, direction).wait_send()

        loop(2, ways)
        pl.when(section == 1)(lambda: send_far(m).wait_send())
        loop(
            NX * (NY - 1),
            lambda k: send_proj(m, k // (NY - 1), k % (NY - 1) + 1).wait_send(),
        )

        @pl.when(section == 0)
        def _():
            loop(NX * NY, lambda k: onward(m, k // NY, k % NY).wait_send())

    loop(MICRO, drain)
    loop(MICRO * 2, lambda k: keep(k // 2, k % 2).wait())

    @pl.when(section == 0)
    def _():
        plane(lambda m, dx, dy: first(m, dx, dy).wait_send())

    @pl.when(section == 0)
    def _():
        ring_drain(in_hop)
        own_out().wait_send()

    pl.when(section == 1)(lambda: ring_drain(out_hop))


def body(
    stream, norm_gain, w_x, w_bc, w_dt, conv_x, conv_bc, dt_bias, decay_rate, skip_d, y_gain, w_out
):
    whole = pl.BlockSpec(memory_space=pltpu.HBM)
    dma = pltpu.SemaphoreType.DMA
    return pl.pallas_call(
        kernel,
        out_shape=jax.ShapeDtypeStruct((1, MICRO, 1, LEN, WIDTH), BF16),
        in_specs=[whole] * 12,
        out_specs=whole,
        scratch_shapes=[
            pltpu.VMEM((MICRO, NX, LEN, 2 * LEN), BF16),
            pltpu.VMEM((1, NX * WIDTH), F32),
            pltpu.VMEM((4, WIDTH + BC), F32),
            pltpu.VMEM((1, 16), F32),
            pltpu.VMEM((1, 16), F32),
            pltpu.VMEM((1, 16), F32),
            pltpu.VMEM((1, WIDTH), F32),
            pltpu.VMEM((NZ * LEN, WIDTH + BC), BF16),
            pltpu.VMEM((WIDTH, NZ * LEN), BF16),
            pltpu.VMEM((WIDTH, NZ * LEN), BF16),
            pltpu.VMEM((LEN, NZ * LEN), BF16),
            pltpu.VMEM((MICRO, NY, ROWS, 2 * LEN), BF16),
            pltpu.VMEM((MICRO, ROWS, WIDTH), BF16),
            pltpu.VMEM((MICRO, ROWS, COLS), BF16),
            pltpu.VMEM((MICRO, 2, LEN, COLS), BF16),
            pltpu.VMEM((MICRO, 2, HALF, COLS), BF16),
            pltpu.VMEM((MICRO, LEN, COLS), BF16),
            pltpu.VMEM((8 + LEN, LEN), F32),
            pltpu.VMEM((LEN, WIDTH + BC), F32),
            pltpu.VMEM((LEN, WIDTH), F32),
            pltpu.VMEM((MICRO, NX, LEN, WIDTH), BF16),
            pltpu.VMEM((MICRO, NY, ROWS, 2 * LEN), BF16),
            pltpu.VMEM((MICRO, NY, ROWS, 2 * LEN), BF16),
            pltpu.VMEM((MICRO, ROWS, 2 * LEN), BF16),
            pltpu.VMEM((MICRO, ROWS, LEN), F32),
            dma((2, 4, CHUNKS)),
            dma((2, 4, CHUNKS)),
            dma((2, 4)),
            dma((2, 4)),
            dma((2, 4, CHUNKS)),
            dma((2, 4, CHUNKS)),
            dma((MICRO, NX, NY)),
            dma((MICRO, NX, NY)),
            dma((MICRO, NX, NY)),
            dma((MICRO, NX, NY)),
            dma((MICRO, 2)),
            dma((MICRO, 2)),
            dma((MICRO,)),
            dma((MICRO,)),
            dma((MICRO, 2, 2)),
            dma((MICRO, 2, 2)),
            dma((MICRO, 2, 2)),
            dma((MICRO, 2, 2)),
            dma((MICRO, 2)),
            dma((MICRO, 2)),
            dma((MICRO, NX, NY)),
            dma((MICRO, NX, NY)),
            dma((MICRO, NX, 2)),
            dma((MICRO, NX, 2)),
            dma((2, 4, CHUNKS)),
            dma((2, 4, CHUNKS)),
            dma((NZ,)),
            dma((NZ,)),
            dma,
            dma,
            dma((11,)),
            dma((MICRO, NX, 2)),
            dma((MICRO, 2)),
            pltpu.SemaphoreType.REGULAR,
        ],
        compiler_params=pltpu.CompilerParams(
            collective_id=0, has_side_effects=True, vmem_limit_bytes=60 * 1024 * 1024
        ),
        name="mixer",
    )(
        stream,
        norm_gain,
        w_x,
        w_bc,
        jnp.swapaxes(w_dt, 1, 2),
        conv_x,
        conv_bc,
        dt_bias,
        decay_rate,
        skip_d,
        y_gain,
        w_out,
    )


def solution(mesh):
    in_specs = (
        P(None, "dp", None, "head"),
        P("section", None),
        P("section", "dp", "head"),
        P("section", "dp", "head"),
        P("section", "dp", "head"),
        P("section", None, "head"),
        P("section", None, "head"),
        P("section", "head"),
        P("section", "head"),
        P("section", "head"),
        P("section", "head"),
        P("section", "head", "dp"),
    )
    out_specs = P("section", None, "dp", None, "head")
    return jax.shard_map(body, mesh=mesh, in_specs=in_specs, out_specs=out_specs, check_vma=False)
```

```python
import functools

import jax
import jax.numpy as jnp
from jax import lax
from jax.experimental import pallas as pl
from jax.experimental.pallas import tpu as pltpu
from jax.sharding import PartitionSpec as P

MESH = pl.DeviceIdType.MESH
HEAD_DIM = 64
STATE = 128
NX = 4
NY = 4
NZ = 8
MICRO = 2
LEN = 128
ROWS = NX * LEN
WIDTH = 1024
BC = 2 * STATE
COLS = WIDTH + BC + 128
CHUNKS = 4
HALF = LEN // 2
EPS = 1e-05
F32 = jnp.float32
BF16 = jnp.bfloat16


def remote(src, dst, send_sem, recv_sem, device):
    return pltpu.make_async_remote_copy(
        src_ref=src,
        dst_ref=dst,
        send_sem=send_sem,
        recv_sem=recv_sem,
        device_id=device,
        device_id_type=MESH,
    )


def kernel(
    stream_ref,
    gain_ref,
    w_x_ref,
    w_bc_ref,
    w_dt_ref,
    conv_x_ref,
    conv_bc_ref,
    bias_ref,
    rate_ref,
    skip_ref,
    y_gain_ref,
    w_out_ref,
    out_ref,
    staged,
    gains,
    taps,
    biases,
    rates,
    skips,
    y_gains,
    w_in,
    w_out,
    relay,
    w_step,
    act,
    scaled,
    part,
    got,
    hop_got,
    far_got,
    padded,
    conv,
    y_raw,
    y_all,
    proj,
    proj_got,
    h_next,
    squares,
    in_send,
    in_recv,
    step_send,
    step_recv,
    wout_send,
    wout_recv,
    first_send,
    first_recv,
    next_send,
    next_recv,
    hop_send,
    hop_recv,
    far_send,
    far_recv,
    part_send,
    part_recv,
    y_send,
    y_recv,
    pass_send,
    pass_recv,
    proj_send,
    proj_recv,
    out_send,
    out_recv,
    relay_send,
    relay_recv,
    push_send,
    push_recv,
    own_send,
    own_recv,
    load_sem,
    stream_sem,
    keep_sem,
    go_sem,
):
    section = lax.axis_index("section")
    dp = lax.axis_index("dp")
    y = lax.axis_index("head")
    z = dp // NX
    x = dp % NX

    def at(s, zz, xx, yy):
        return (s, zz * NX + xx, yy)

    right, left = (z + 1) % NZ, (z + NZ - 1) % NZ
    sibling = at(1 - section, z, x, y)
    own_block = pl.ds(pl.multiple_of(z * LEN, LEN), LEN)

    loads = [
        pltpu.make_async_copy(source, target, load_sem.at[i])
        for i, (source, target) in enumerate(
            [
                (w_out_ref.at[0], w_out.at[:, own_block]),
                (w_x_ref.at[0], w_in.at[own_block, :WIDTH]),
                (w_bc_ref.at[0], w_in.at[own_block, WIDTH : WIDTH + BC]),
                (w_dt_ref.at[0], w_step.at[:16, own_block]),
                (gain_ref, gains),
                (conv_x_ref.at[0], taps.at[:, :WIDTH]),
                (conv_bc_ref.at[0], taps.at[:, WIDTH:]),
                (bias_ref, biases),
                (rate_ref, rates),
                (skip_ref, skips),
                (y_gain_ref, y_gains),
            ]
        )
    ]
    for load in loads:
        load.start()

    def stage(m, xx, half):
        return pltpu.make_async_copy(
            stream_ref.at[m, 0, :, pl.ds(pl.multiple_of((xx + NX * half) * LEN, LEN), LEN)],
            staged.at[m, xx, :, pl.ds(half * LEN, LEN)],
            stream_sem.at[m, xx, half],
        )

    @pl.when(section == 0)
    def _():
        def work(i, carry):
            for half in range(2):
                stage(i // NX, i % NX, half).start()
            return carry

        lax.fori_loop(0, MICRO * NX, work, 0)

    barrier = pltpu.get_barrier_semaphore()
    for dx in range(NX):
        for dy in range(NY):
            if dx or dy:
                pl.semaphore_signal(
                    barrier,
                    inc=1,
                    device_id=at(section, z, (x + dx) % NX, (y + dy) % NY),
                    device_id_type=MESH,
                )
    for dy in range(NY):
        pl.semaphore_signal(
            barrier, inc=1, device_id=at(1 - section, z, x, (y + dy) % NY), device_id_type=MESH
        )
    for zz in (right, left):
        pl.semaphore_signal(
            barrier, inc=1, device_id=at(section, zz, x, y), device_id_type=MESH
        )
    pl.semaphore_wait(barrier, NX * NY - 1 + NY + 2)

    def hop(buffer, by_rows, sends, receives):
        def one(direction, step, chunk):
            owner = (z + NZ - step) % NZ if direction == 0 else (z + step) % NZ
            if by_rows:
                size = LEN // CHUNKS
                piece = buffer.at[pl.ds(pl.multiple_of(owner * LEN + chunk * size, size), size)]
            else:
                size = WIDTH // CHUNKS
                piece = buffer.at[
                    pl.ds(chunk * size, size), pl.ds(pl.multiple_of(owner * LEN, LEN), LEN)
                ]
            return remote(
                piece,
                piece,
                sends.at[direction, step, chunk],
                receives.at[direction, step, chunk],
                at(section, right if direction == 0 else left, x, y),
            )

        return one

    def step_hop(direction, step):
        owner = (z + NZ - step) % NZ if direction == 0 else (z + step) % NZ
        piece = w_step.at[:16, pl.ds(pl.multiple_of(owner * LEN, LEN), LEN)]
        return remote(
            piece,
            piece,
            step_send.at[direction, step],
            step_recv.at[direction, step],
            at(section, right if direction == 0 else left, x, y),
        )

    in_hop = hop(w_in, True, in_send, in_recv)
    out_hop = hop(w_out, False, wout_send, wout_recv)
    relay_hop = hop(relay, False, relay_send, relay_recv)

    def loop(count, work):
        def one(i, carry):
            work(i)
            return carry

        lax.fori_loop(0, count, one, 0)

    def ring_start(one):
        if one is in_hop:
            for direction in range(2):
                step_hop(direction, 0).start()

        def work(chunk):
            for direction in range(2):
                one(direction, 0, chunk).start()

        loop(CHUNKS, work)

    def ring_step(one, step):
        if one is in_hop:
            for direction in range(2):
                step_hop(direction, step - 1).wait_recv()
                step_hop(direction, step).start()

        def work(chunk):
            for direction in range(2):
                one(direction, step - 1, chunk).wait_recv()
                one(direction, step, chunk).start()

        loop(CHUNKS, work)

    def ring_last(one):
        if one is in_hop:
            for direction in range(2):
                step_hop(direction, 2).wait_recv()
            step_hop(0, 3).start()

        def work(chunk):
            for direction in range(2):
                one(direction, 2, chunk).wait_recv()
                pl.when(chunk // (CHUNKS // 2) == direction)(
                    lambda direction=direction: one(direction, 3, chunk).start()
                )

        loop(CHUNKS, work)

    def ring_middle(one, arrived=None):
        def work(i):
            ring_step(one, i + 1)
            if arrived is not None:
                arrived(i + 1)

        loop(2, work)
        ring_last(one)
        if arrived is not None:
            arrived(3)

    def ring_end(one):
        if one is in_hop:
            step_hop(0, 3).wait_recv()
        for direction in range(2):
            loop(
                CHUNKS // 2,
                lambda i, direction=direction: one(
                    direction, 3, direction * (CHUNKS // 2) + i
                ).wait_recv(),
            )

    def ring_drain(one):
        if one is in_hop:
            for step in range(4):
                for direction in range(2 if step < 3 else 1):
                    step_hop(direction, step).wait_send()

        def work(i):
            for direction in range(2):
                one(direction, i // CHUNKS, i % CHUNKS).wait_send()

        loop(3 * CHUNKS, work)
        for direction in range(2):
            loop(
                CHUNKS // 2,
                lambda i, direction=direction: one(
                    direction, 3, direction * (CHUNKS // 2) + i
                ).wait_send(),
            )

    def own_out():
        return remote(
            w_out.at[:, own_block], relay.at[:, own_block], own_send, own_recv, sibling
        )

    def push(step):
        columns = pl.ds(pl.multiple_of((z + step) % NZ * LEN, LEN), LEN)
        return remote(
            relay.at[:, columns],
            w_out.at[:, columns],
            push_send.at[step],
            push_recv.at[step],
            sibling,
        )

    def push_both(step):
        push(step).start()
        push(NZ - step).start()

    loads[0].wait()

    @pl.when(section == 0)
    def _():
        own_out().start()

    for load in loads[1:]:
        load.wait()
    w_step[16:, :] = jnp.zeros((LEN - 16, NZ * LEN), BF16)
    def first(m, dx, dy):
        to_x = (x + dx) % NX
        to_y = (y + dy) % NY
        return remote(
            staged.at[m, to_x],
            act.at[m, y, pl.ds(pl.multiple_of(x * LEN, LEN), LEN), :],
            first_send.at[m, dx, dy],
            first_recv.at[m, dx, dy],
            at(0, z, to_x, to_y),
        )

    def block(ahead):
        return pl.ds(pl.multiple_of((x + ahead) % NX * LEN, LEN), LEN)

    def order(i):
        return i + i // 2 - i // 3 * 2

    def onward(m, ahead, dy):
        return remote(
            h_next.at[m, block(ahead), :],
            act.at[m, y, block(ahead), :],
            next_send.at[m, ahead, dy],
            next_recv.at[m, ahead, dy],
            at(1 - section, z, x, (y + dy) % NY),
        )

    def towards(direction):
        return at(section, z, (x + 1 + 2 * direction) % NX, y)

    def half_block(ahead, half):
        return pl.ds(pl.multiple_of((x + ahead) % NX * LEN + half * HALF, HALF), HALF)

    def send_hop(m, direction):
        return remote(
            part.at[m, half_block(2, direction), :],
            hop_got.at[m, direction],
            hop_send.at[m, direction],
            hop_recv.at[m, direction],
            towards(direction),
        )

    def send_far(m):
        return remote(
            part.at[m, block(2), :],
            far_got.at[m],
            far_send.at[m],
            far_recv.at[m],
            at(section, z, (x + 2) % NX, y),
        )

    def send_part(m, direction, half):
        return remote(
            part.at[m, half_block(1 + 2 * direction, half), :],
            got.at[m, direction, pl.ds(half * HALF, HALF), :],
            part_send.at[m, direction, half],
            part_recv.at[m, direction, half],
            towards(direction),
        )

    def fold(m):
        for direction in range(2):
            send_hop(m, direction).wait_recv()
            rows = half_block(1 + 2 * direction, direction)
            for c in range(COLS // LEN):
                cols = slice(c * LEN, (c + 1) * LEN)
                part[m, rows, cols] = (
                    part[m, rows, cols].astype(F32) + hop_got[m, direction, :, cols].astype(F32)
                ).astype(BF16)
            send_part(m, direction, direction).start()

    def send_y(m, direction, half):
        piece = y_all.at[m, x, pl.ds(half * HALF, HALF), :]
        return remote(
            piece,
            piece,
            y_send.at[m, direction, half],
            y_recv.at[m, direction, half],
            towards(direction),
        )

    def pass_y(m, direction):
        piece = y_all.at[m, (x + 3 - 2 * direction) % NX, pl.ds(direction * HALF, HALF), :]
        return remote(
            piece,
            piece,
            pass_send.at[m, direction],
            pass_recv.at[m, direction],
            towards(direction),
        )

    def pass_on(m):
        for direction in range(2):
            send_y(m, direction, direction).wait_recv()
            pass_y(m, direction).start()

    def wait_y(m, ahead):
        @pl.when(ahead == 1)
        def _():
            send_y(m, 1, 0).wait_recv()

        @pl.when(ahead == 3)
        def _():
            send_y(m, 0, 1).wait_recv()

        @pl.when(ahead == 2)
        def _():
            for direction in range(2):
                pass_y(m, direction).wait_recv()

    def send_proj(m, ahead, dy):
        to_y = (y + dy) % NY
        return remote(
            proj.at[m, to_y, block(ahead), :],
            proj_got.at[m, dy, block(ahead), :],
            proj_send.at[m, ahead, dy],
            proj_recv.at[m, ahead, dy],
            at(section, z, x, to_y),
        )

    def send_out(m, ahead, half):
        return remote(
            h_next.at[m, block(ahead), pl.ds(half * LEN, LEN)],
            out_ref.at[0, m, 0, :, pl.ds(pl.multiple_of((x + NX * half) * LEN, LEN), LEN)],
            out_send.at[m, ahead, half],
            out_recv.at[m, ahead, half],
            at(section, z, (x + ahead) % NX, y),
        )

    lane = lax.broadcasted_iota(jnp.int32, (LEN, LEN), 1)
    row = lax.broadcasted_iota(jnp.int32, (LEN, LEN), 0)

    def prepare(m, ahead):
        def scale(i, carry):
            rows = pl.ds(pl.multiple_of((x + ahead) % NX * LEN + i * 64, 64), 64)
            total = jnp.zeros((64, LEN), F32)
            for yy in range(NY):
                for half in range(2):
                    at_ = yy * 2 * LEN + half * LEN
                    value = act[m, yy, rows, half * LEN : (half + 1) * LEN].astype(F32)
                    total = total + value * value
                    gain = gains[
                        :, pl.ds(pl.multiple_of((yy * 2 + half) * NX * LEN + x * LEN, LEN), LEN)
                    ]
                    scaled[m, rows, at_ : at_ + LEN] = (value * gain).astype(BF16)
            squares[m, rows, :] = jnp.broadcast_to(
                jnp.sum(total, axis=1, keepdims=True), (64, LEN)
            )
            return carry

        lax.fori_loop(0, LEN // 64, scale, 0)

    def project_in(m, ahead):
        rows = block(ahead)
        values = scaled[m, rows, :]
        for c in range((WIDTH + BC) // 256):
            cols = slice(c * 256, (c + 1) * 256)
            part[m, rows, cols] = jnp.dot(
                values, w_in[:, cols], preferred_element_type=F32
            ).astype(BF16)
        small = lax.dot_general(
            values, w_step[...], (((1,), (1,)), ((), ())), preferred_element_type=F32
        )
        high = small.astype(BF16).astype(F32)
        low = small - high
        square = squares[m, rows, :]
        square_high = square.astype(BF16).astype(F32)
        packed = high + pltpu.roll(low, 16, 1)
        packed = jnp.where(lane == 32, square_high, packed)
        packed = jnp.where(lane == 33, square - square_high, packed)
        part[m, rows, WIDTH + BC :] = packed.astype(BF16)

        @pl.when(ahead == 2)
        def _():
            @pl.when(section == 0)
            def _():
                for direction in range(2):
                    send_hop(m, direction).start()

            pl.when(section == 1)(lambda: send_far(m).start())

        for direction in range(2):

            @pl.when(ahead == 1 + 2 * direction)
            def _(direction=direction):
                send_part(m, direction, 1 - direction).start()
                pl.when(section == 1)(lambda: send_part(m, direction, direction).start())

    def mix(m):
        for half in range(2):
            for direction in range(2):
                send_part(m, direction, half).wait_recv()
        pl.when(section == 1)(lambda: send_far(m).wait_recv())
        own = block(0)

        def summed(cols):
            total = part[m, own, cols].astype(F32) + far_got[m, :, cols].astype(F32)
            for direction in range(2):
                total = total + got[m, direction, :, cols].astype(F32)
            return total

        tail = summed(slice(WIDTH + BC, COLS))
        square = tail[:, 32:33] + tail[:, 33:34]
        inverse = lax.rsqrt(square * (1.0 / (NX * WIDTH)) + EPS)
        raw = (tail + pltpu.roll(tail, LEN - 16, 1)) * inverse
        pre = raw + jnp.concatenate([biases[...], jnp.zeros((1, LEN - 16), F32)], axis=1)
        steps = jnp.maximum(pre, 0.0) + jnp.log1p(jnp.exp(-jnp.abs(pre)))
        steps = jnp.where(lane < 16, steps, 0.0)
        lower = jnp.where(row >= lane, 1.0, 0.0)
        decay = jnp.dot(
            lower,
            steps * jnp.concatenate([rates[...], jnp.zeros((1, LEN - 16), F32)], axis=1),
            precision=lax.Precision.HIGHEST,
            preferred_element_type=F32,
        )
        decay_t = decay.T
        inverse_wide = jnp.broadcast_to(inverse, (LEN, LEN))

        padded[0:8, :] = jnp.zeros((8, LEN), F32)

        for c in range((WIDTH + BC) // LEN):
            cols = slice(c * LEN, (c + 1) * LEN)
            padded[8:, :] = summed(cols) * inverse_wide
            value = jnp.zeros((LEN, LEN), F32)
            for tap in range(4):
                value = value + taps[tap : tap + 1, cols] * padded[5 + tap : 5 + tap + LEN, :]
            conv[:, cols] = value / (1.0 + jnp.exp(-value))

        scores = lax.dot_general(
            conv[:, WIDTH + STATE : WIDTH + BC],
            conv[:, WIDTH : WIDTH + STATE],
            (((1,), (1,)), ((), ())),
            precision=lax.Precision.HIGHEST,
            preferred_element_type=F32,
        )
        scores = jnp.where(row >= lane, scores, 0.0)
        power = jnp.zeros((LEN, LEN), F32)
        for pair in range(WIDTH // LEN):
            cols = slice(pair * LEN, (pair + 1) * LEN)
            mixes = []
            for j in (2 * pair, 2 * pair + 1):
                gap = jnp.minimum(decay_t[j : j + 1, :] - decay[:, j : j + 1], 0.0)
                mixes.append((jnp.exp(gap) * scores).astype(BF16))
            value = conv[:, cols]
            step = jnp.where(
                lane < HEAD_DIM,
                steps[:, 2 * pair : 2 * pair + 1],
                steps[:, 2 * pair + 1 : 2 * pair + 2],
            )
            stepped = value * step
            blocks = jnp.concatenate(
                [
                    jnp.where(lane < HEAD_DIM, stepped, 0.0).astype(BF16),
                    jnp.where(lane < HEAD_DIM, 0.0, stepped).astype(BF16),
                ],
                axis=0,
            )
            mixed = jnp.dot(
                jnp.concatenate(mixes, axis=1), blocks, preferred_element_type=F32
            )
            skip = jnp.where(
                lane[:1] < HEAD_DIM,
                skips[:, 2 * pair : 2 * pair + 1],
                skips[:, 2 * pair + 1 : 2 * pair + 2],
            )
            mixed = mixed + skip * value
            power = power + mixed * mixed
            y_raw[:, cols] = mixed
        norm = lax.rsqrt(jnp.sum(power, axis=1, keepdims=True) * (1.0 / WIDTH) + EPS)
        norm = jnp.broadcast_to(norm, (LEN, LEN))
        for c in range(WIDTH // LEN):
            cols = slice(c * LEN, (c + 1) * LEN)
            y_all[m, x, :, cols] = (y_raw[:, cols] * norm * y_gains[:, cols]).astype(BF16)
        for half in range(2):
            for direction in range(2):
                send_y(m, direction, (direction + half) % 2).start()

    def project_out(m, ahead):
        values = y_all[m, (x + ahead) % NX]
        for dy in (2, 1, 3, 0):
            to_y = (y + dy) % NY
            cols = pl.ds(pl.multiple_of(to_y * 2 * LEN, 2 * LEN), 2 * LEN)
            proj[m, to_y, block(ahead), :] = jnp.dot(
                values, w_out[:, cols], preferred_element_type=F32
            ).astype(BF16)
            if dy:
                send_proj(m, ahead, dy).start()

    def keep(m, half):
        return pltpu.make_async_copy(
            h_next.at[m, block(0), pl.ds(half * LEN, LEN)],
            out_ref.at[0, m, 0, :, pl.ds(pl.multiple_of((x + NX * half) * LEN, LEN), LEN)],
            keep_sem.at[m, half],
        )

    def give(m, ahead):
        rows = block(ahead)

        @pl.when(ahead != 0)
        def _():
            for half in range(2):
                send_out(m, ahead, half).start()

        @pl.when(ahead == 0)
        def _():
            for half in range(2):
                keep(m, half).start()

    def finish(m, ahead):
        for dy in (1, 3, 2):
            send_proj(m, ahead, dy).wait_recv()
        rows = block(ahead)
        total = proj[m, y, rows, :].astype(F32)
        for dy in (1, 2, 3):
            total = total + proj_got[m, dy, rows, :].astype(F32)
        h_next[m, rows, :] = (act[m, y, rows, :].astype(F32) + total).astype(BF16)

        @pl.when(section == 0)
        def _():
            for dy in (2, 1, 3, 0):
                onward(m, ahead, dy).start()

        pl.when(section == 1)(lambda: give(m, ahead))

    def plane(work):
        def one(i, carry):
            pl.when(i % (NX * NY) != 0)(
                lambda: work(i // (NX * NY), i // NY % NX, i % NY)
            )
            return carry

        lax.fori_loop(0, MICRO * NX * NY, one, 0)

    @pl.when(section == 1)
    def _():
        own_out().wait_recv()
        pl.semaphore_wait(go_sem, 1)
        ring_start(relay_hop)
        ring_middle(relay_hop, push_both)

    ring_start(in_hop)

    @pl.when(section == 0)
    def _():
        def arrange(m):
            def work(xx):
                for half in range(2):
                    stage(m, xx, half).wait()

            loop(NX, work)
            act[m, y, pl.ds(pl.multiple_of(x * LEN, LEN), LEN), :] = staged[m, x]

        loop(MICRO, arrange)
        plane(lambda m, dx, dy: first(m, dx, dy).start())
        for m in range(MICRO):
            far_got[m] = jnp.zeros((LEN, COLS), BF16)

    @pl.when(section == 1)
    def _():
        ring_end(relay_hop)
        push(NZ // 2).start()

    ring_middle(in_hop)

    @pl.when(section == 0)
    def _():
        pl.semaphore_signal(go_sem, inc=1, device_id=sibling, device_id_type=MESH)
        plane(lambda m, dx, dy: first(m, dx, dy).wait_recv())
        loop(MICRO * NX, lambda i: prepare(i // NX, i % NX))

    @pl.when(section == 1)
    def _():
        ring_start(out_hop)
        ring_drain(relay_hop)
        loop(NZ - 1, lambda step: push(step + 1).wait_send())

    ring_end(in_hop)
    pl.when(section == 1)(lambda: ring_drain(in_hop))

    def rows_in(i, carry):
        m = i // NX
        turn = i % NX
        ahead = order(jnp.where(section == 0, NX - 1 - turn, turn))

        @pl.when(section == 1)
        def _():
            for dy in range(NY):
                onward(m, ahead, dy).wait_recv()
            prepare(m, ahead)

        project_in(m, ahead)
        return carry

    def rows_and_more(i):
        rows_in(i, 0)
        pl.when(jnp.logical_and(section == 0, jnp.logical_or(i == NX, i == MICRO * NX - 1)))(
            lambda: fold(jnp.where(i == NX, 0, 1))
        )

        @pl.when(section == 1)
        def _():
            pl.when(jnp.logical_or(i == NX - 1, i == NX))(lambda: ring_step(out_hop, i - 2))
            pl.when(i == MICRO * NX - 1)(lambda: ring_last(out_hop))

    loop(MICRO * NX, rows_and_more)

    def unit(i):
        behind = jnp.maximum(i - 2, 0)
        return (
            jnp.where(i < 2, i, behind // (NX - 1)),
            jnp.where(i < 2, 0, order(behind % (NX - 1) + 1)),
        )

    def ended(i):
        return jnp.where(
            i < 1, 0, jnp.where(i < 4, 1, jnp.where(i < 6, 4, jnp.where(i < 7, 5, 8)))
        )

    def stage_out(i):
        m, ahead = unit(i)

        @pl.when(i < 2)
        def _():
            mix(m)

            @pl.when(m == 0)
            def _():
                @pl.when(section == 0)
                def _():
                    loop(NZ - 1, lambda step: push(step + 1).wait_recv())

                @pl.when(section == 1)
                def _():
                    ring_end(out_hop)

        @pl.when(i >= 2)
        def _():
            wait_y(m, ahead)

        project_out(m, ahead)
        pl.when(
            jnp.logical_or(i == jnp.where(section == 0, 1, 0), i == 4)
        )(lambda: pass_on(jnp.where(i == 4, 1, 0)))

        def end(k, carry):
            finish(*unit(k))
            return carry

        lax.fori_loop(ended(i - 1), ended(i), end, 0)

    loop(MICRO * NX, stage_out)

    @pl.when(section == 0)
    def _():
        def later(i, carry):
            give(i // NX, i % NX)
            return carry

        lax.fori_loop(0, MICRO * NX, later, 0)

    def drain(m):
        def outs(k):
            for half in range(2):
                send_out(m, k + 1, half).wait()

        loop(NX - 1, outs)

        def ways(direction):
            for half in range(2):
                send_part(m, direction, half).wait_send()
                send_y(m, direction, half).wait_send()
            pl.when(section == 0)(lambda: send_hop(m, direction).wait_send())
            pass_y(m, direction).wait_send()

        loop(2, ways)
        pl.when(section == 1)(lambda: send_far(m).wait_send())
        loop(
            NX * (NY - 1),
            lambda k: send_proj(m, k // (NY - 1), k % (NY - 1) + 1).wait_send(),
        )

        @pl.when(section == 0)
        def _():
            loop(NX * NY, lambda k: onward(m, k // NY, k % NY).wait_send())

    loop(MICRO, drain)
    loop(MICRO * 2, lambda k: keep(k // 2, k % 2).wait())

    @pl.when(section == 0)
    def _():
        plane(lambda m, dx, dy: first(m, dx, dy).wait_send())

    @pl.when(section == 0)
    def _():
        ring_drain(in_hop)
        own_out().wait_send()

    pl.when(section == 1)(lambda: ring_drain(out_hop))


def body(
    stream, norm_gain, w_x, w_bc, w_dt, conv_x, conv_bc, dt_bias, decay_rate, skip_d, y_gain, w_out
):
    whole = pl.BlockSpec(memory_space=pltpu.HBM)
    dma = pltpu.SemaphoreType.DMA
    return pl.pallas_call(
        kernel,
        out_shape=jax.ShapeDtypeStruct((1, MICRO, 1, LEN, WIDTH), BF16),
        in_specs=[whole] * 12,
        out_specs=whole,
        scratch_shapes=[
            pltpu.VMEM((MICRO, NX, LEN, 2 * LEN), BF16),
            pltpu.VMEM((1, NX * WIDTH), F32),
            pltpu.VMEM((4, WIDTH + BC), F32),
            pltpu.VMEM((1, 16), F32),
            pltpu.VMEM((1, 16), F32),
            pltpu.VMEM((1, 16), F32),
            pltpu.VMEM((1, WIDTH), F32),
            pltpu.VMEM((NZ * LEN, WIDTH + BC), BF16),
            pltpu.VMEM((WIDTH, NZ * LEN), BF16),
            pltpu.VMEM((WIDTH, NZ * LEN), BF16),
            pltpu.VMEM((LEN, NZ * LEN), BF16),
            pltpu.VMEM((MICRO, NY, ROWS, 2 * LEN), BF16),
            pltpu.VMEM((MICRO, ROWS, WIDTH), BF16),
            pltpu.VMEM((MICRO, ROWS, COLS), BF16),
            pltpu.VMEM((MICRO, 2, LEN, COLS), BF16),
            pltpu.VMEM((MICRO, 2, HALF, COLS), BF16),
            pltpu.VMEM((MICRO, LEN, COLS), BF16),
            pltpu.VMEM((8 + LEN, LEN), F32),
            pltpu.VMEM((LEN, WIDTH + BC), F32),
            pltpu.VMEM((LEN, WIDTH), F32),
            pltpu.VMEM((MICRO, NX, LEN, WIDTH), BF16),
            pltpu.VMEM((MICRO, NY, ROWS, 2 * LEN), BF16),
            pltpu.VMEM((MICRO, NY, ROWS, 2 * LEN), BF16),
            pltpu.VMEM((MICRO, ROWS, 2 * LEN), BF16),
            pltpu.VMEM((MICRO, ROWS, LEN), F32),
            dma((2, 4, CHUNKS)),
            dma((2, 4, CHUNKS)),
            dma((2, 4)),
            dma((2, 4)),
            dma((2, 4, CHUNKS)),
            dma((2, 4, CHUNKS)),
            dma((MICRO, NX, NY)),
            dma((MICRO, NX, NY)),
            dma((MICRO, NX, NY)),
            dma((MICRO, NX, NY)),
            dma((MICRO, 2)),
            dma((MICRO, 2)),
            dma((MICRO,)),
            dma((MICRO,)),
            dma((MICRO, 2, 2)),
            dma((MICRO, 2, 2)),
            dma((MICRO, 2, 2)),
            dma((MICRO, 2, 2)),
            dma((MICRO, 2)),
            dma((MICRO, 2)),
            dma((MICRO, NX, NY)),
            dma((MICRO, NX, NY)),
            dma((MICRO, NX, 2)),
            dma((MICRO, NX, 2)),
            dma((2, 4, CHUNKS)),
            dma((2, 4, CHUNKS)),
            dma((NZ,)),
            dma((NZ,)),
            dma,
            dma,
            dma((11,)),
            dma((MICRO, NX, 2)),
            dma((MICRO, 2)),
            pltpu.SemaphoreType.REGULAR,
        ],
        compiler_params=pltpu.CompilerParams(
            collective_id=0, has_side_effects=True, vmem_limit_bytes=60 * 1024 * 1024
        ),
        name="mixer",
    )(
        stream,
        norm_gain,
        w_x,
        w_bc,
        jnp.swapaxes(w_dt, 1, 2),
        conv_x,
        conv_bc,
        dt_bias,
        decay_rate,
        skip_d,
        y_gain,
        w_out,
    )


def solution(mesh):
    in_specs = (
        P(None, "dp", None, "head"),
        P("section", None),
        P("section", "dp", "head"),
        P("section", "dp", "head"),
        P("section", "dp", "head"),
        P("section", None, "head"),
        P("section", None, "head"),
        P("section", "head"),
        P("section", "head"),
        P("section", "head"),
        P("section", "head"),
        P("section", "head", "dp"),
    )
    out_specs = P("section", None, "dp", None, "head")
    return jax.shard_map(body, mesh=mesh, in_specs=in_specs, out_specs=out_specs, check_vma=False)
```
